256 devices in a mesh: row: 8 (over z_lo, core), col: 32 (over x, z_hi, y).
Axes of the slice: x: 4, y: 4, z: 8 (z_hi: 2, z_lo: 4; z = z_hi * 4 + z_lo), core: 2. Of those that a mesh axis runs over, the one named last changes fastest.
Arguments:
- pair_rep: bfloat16 [1024, 1024, 128], P('row', 'col'), may hold values from -6 to 6
- residue_mask: int32 [1024], replicated, may hold values 0 or 1
- in_gain: float32 [128], replicated, may hold values from 0.25 to 1.75
- in_bias: float32 [128], replicated, may hold values from -3 to 3
- in_weights: bfloat16 [4, 128, 128], replicated, may hold values from -3 to 3
- gate_weight: bfloat16 [128, 128], replicated, may hold values from -0.5 to 0.5
- out_gain: float32 [128], replicated, may hold values from 0.25 to 1.75
- out_bias: float32 [128], replicated, may hold values from -3 to 3
- out_weight: bfloat16 [128, 128], replicated, may hold values from -0.5 to 0.5
Outputs:
- update: bfloat16 [1024, 1024, 128], P('row', 'col')
The draws below stay inside these ranges and needn't reach their ends.
All inputs are finite; a program needn't handle non-finite values.
Results may differ from the reference program's by a relative error of at most 0.0057.
Values may be sent and summed in bfloat16 or wider, within the bound.
No kernel may reach another device: no remote copies, remote signals or barrier semaphores. Data moves between devices by JAX's collectives and lax.ppermute only.
A program may use at most 128 MiB of HBM per device.

```python
import math
import jax
import jax.numpy as jnp
from jax import lax

C = 128
H = 128
N = 1024


def draw_in_weights(key, part):
    key = jax.random.fold_in(key, 11)
    key_one, key_two = jax.random.split(key)
    spread = jnp.exp(jax.random.uniform(key_two, (4, 1, H), jnp.float32, math.log(0.8), math.log(1.25)))
    entries = jnp.clip(jax.random.normal(key_one, (4, C, H), jnp.float32), -3.0, 3.0)
    return (entries * spread / math.sqrt(C)).astype(jnp.bfloat16)


def plant(drawn, rng, low, high):
    longest = drawn.shape.index(max(drawn.shape))
    spots = []
    for shift in (0, 1):
        where = [jax.random.randint(jax.random.fold_in(rng, axis), (), 0, length) for axis, length in enumerate(drawn.shape)]
        where[longest] = (where[longest] + shift) % drawn.shape[longest]
        spots.append(tuple(where))
    return drawn.at[spots[0]].set(low).at[spots[1]].set(high)


def block_scale(rng, extent, pieces, smallest, largest):
    loudness, own = 1.0, jax.random.fold_in(rng, 6)
    for position, shards_of in pieces:
        draws = jnp.exp(jax.random.uniform(jax.random.fold_in(own, position), (shards_of,), jnp.float32, smallest / len(pieces), largest / len(pieces)))
        loudness = loudness * jnp.repeat(draws, extent[position] // shards_of).reshape([-1 if axis == position else 1 for axis in range(len(extent))])
    return loudness


def noise(key, shape, scale, reach, pieces=(), kind=jnp.bfloat16):
    values = scale * jax.random.normal(key, shape, jnp.float32)
    if pieces:
        values = values * block_scale(key, shape, pieces, -0.22, 0.18)
    return jnp.clip(values, -reach, reach).astype(kind)


def setup_inputs(seed: int = 0) -> dict:
    seeds = jax.random.split(jax.random.key(seed), 10)
    pair_rep = noise(seeds[0], (N, N, C), 1.0, 6.0, ((0, 8), (1, 32)))
    residue_mask = plant((jax.random.randint(seeds[1], (N,), 0, 8) < 7).astype(jnp.int32), jax.random.fold_in(seeds[1], 1), 0, 1)
    in_gain = jnp.clip(1.0 + 0.15 * jax.random.normal(seeds[2], (C,), jnp.float32), 0.25, 1.75)
    in_bias = noise(seeds[3], (C,), 0.5, 3.0, (), jnp.float32)
    in_weights = draw_in_weights(jax.random.fold_in(seeds[9], 71), 0)
    gate_weight = noise(seeds[5], (C, C), C ** -0.5, 0.5)
    out_gain = jnp.clip(1.0 + 0.15 * jax.random.normal(seeds[6], (H,), jnp.float32), 0.25, 1.75)
    out_bias = noise(seeds[7], (H,), 0.5, 3.0, (), jnp.float32)
    out_weight = noise(seeds[8], (H, C), H ** -0.5, 0.5)
    return {"pair_rep": pair_rep, "residue_mask": residue_mask, "in_gain": in_gain, "in_bias": in_bias, "in_weights": in_weights, "gate_weight": gate_weight, "out_gain": out_gain, "out_bias": out_bias, "out_weight": out_weight}


def layer_norm(values, gain_vec, offset, axis_dim):
    average = lax.optimization_barrier(jnp.mean(values, axis=axis_dim, keepdims=True))
    centred = values - average
    spread = lax.optimization_barrier(jnp.mean(centred * centred, axis=axis_dim, keepdims=True))
    return centred * lax.rsqrt(spread + 1e-05) * gain_vec + offset

def reference(pair_rep, residue_mask, in_gain, in_bias, in_weights, gate_weight, out_gain, out_bias, out_weight):
    row_block = math.gcd(N, 64)
    block_count = N // row_block
    mask_float = residue_mask.astype(jnp.float32)
    joined = jnp.concatenate([in_weights[0], in_weights[1], in_weights[2], in_weights[3]], axis=1)

    def normed_rows(first_row):
        pair_rows = lax.dynamic_slice_in_dim(pair_rep, first_row, row_block, 0).astype(jnp.float32)
        return layer_norm(pair_rows, in_gain, in_bias, 2).astype(jnp.bfloat16)

    def factors(block_index):
        first_row = (block_index * row_block).astype(jnp.int32)
        normed_in = normed_rows(first_row)
        projected = jnp.dot(normed_in.reshape(row_block * N, C), joined, preferred_element_type=jnp.float32)
        projected = projected.reshape(row_block, N, 4 * H)
        mask_rows = lax.dynamic_slice_in_dim(mask_float, first_row, row_block, 0)
        pair_mask = (mask_rows[:, None] * mask_float[None, :])[:, :, None]
        left_rows = jax.nn.sigmoid(projected[:, :, :H]) * projected[:, :, H:2 * H] * pair_mask
        right_rows = jax.nn.sigmoid(projected[:, :, 2 * H:3 * H]) * projected[:, :, 3 * H:] * pair_mask
        return (left_rows.astype(jnp.bfloat16).transpose(2, 0, 1), right_rows.astype(jnp.bfloat16).transpose(2, 0, 1))
    left_blocks, right_blocks = lax.map(factors, jnp.arange(block_count, dtype=jnp.int32))
    left_all = left_blocks.transpose(1, 0, 2, 3).reshape(H, N, N)
    right_all = right_blocks.transpose(1, 0, 2, 3).reshape(H, N, N)

    def channel_product(operands):
        return jnp.dot(operands[0], operands[1].T, preferred_element_type=jnp.float32).astype(jnp.bfloat16)
    triangle = lax.map(channel_product, (left_all, right_all))

    def finish(block_index):
        first_row = (block_index * row_block).astype(jnp.int32)
        normed_in = normed_rows(first_row)
        gate_term = jnp.dot(normed_in.reshape(row_block * N, C), gate_weight, preferred_element_type=jnp.float32)
        tri_rows = lax.dynamic_slice_in_dim(triangle, first_row, row_block, 1).astype(jnp.float32)
        normed_out = layer_norm(tri_rows.transpose(1, 2, 0), out_gain, out_bias, 2).astype(jnp.bfloat16)
        out_proj = jnp.dot(normed_out.reshape(row_block * N, H), out_weight, preferred_element_type=jnp.float32)
        return (jax.nn.sigmoid(gate_term) * out_proj).astype(jnp.bfloat16).reshape(row_block, N, C)
    update = lax.map(finish, jnp.arange(block_count, dtype=jnp.int32))
    return update.reshape(N, N, C)
```

```python
import jax
import jax.numpy as jnp
from jax import lax
from jax.sharding import Mesh
from jax.sharding import PartitionSpec as P

CHIPS = ("zl", "x", "zh", "y")


def layer_norm(values, gain_vec, offset, axis_dim):
    average = jnp.mean(values, axis=axis_dim, keepdims=True)
    centred = values - average
    spread = jnp.mean(centred * centred, axis=axis_dim, keepdims=True)
    return centred * lax.rsqrt(spread + 1e-05) * gain_vec + offset


def swap(chunks):
    return lax.all_to_all(chunks, CHIPS, split_axis=0, concat_axis=0, tiled=True)


def local(
    pair_rep,
    residue_mask,
    in_gain,
    in_bias,
    in_weights,
    gate_weight,
    out_gain,
    out_bias,
    out_weight,
):
    rows_here, cols_here, channels = pair_rep.shape
    hidden = in_weights.shape[2]
    row_mask = lax.dynamic_slice_in_dim(
        residue_mask, lax.axis_index(("zl", "core")) * rows_here, rows_here, 0
    ).astype(jnp.float32)
    col_mask = lax.dynamic_slice_in_dim(
        residue_mask, lax.axis_index(("x", "zh", "y")) * cols_here, cols_here, 0
    ).astype(jnp.float32)
    normed_in = layer_norm(pair_rep.astype(jnp.float32), in_gain, in_bias, 2).astype(jnp.bfloat16)
    flattened = normed_in.reshape(rows_here * cols_here, channels)
    joined = jnp.concatenate(
        [in_weights[0], in_weights[1], in_weights[2], in_weights[3], gate_weight], axis=1
    )
    projected = jnp.dot(flattened, joined, preferred_element_type=jnp.float32)
    projected = projected.reshape(rows_here, cols_here, 4 * hidden + channels)
    pair_mask = (row_mask[:, None] * col_mask[None, :])[:, :, None]
    left_tile = (
        jax.nn.sigmoid(projected[:, :, :hidden]) * projected[:, :, hidden : 2 * hidden] * pair_mask
    )
    right_tile = (
        jax.nn.sigmoid(projected[:, :, 2 * hidden : 3 * hidden])
        * projected[:, :, 3 * hidden : 4 * hidden]
        * pair_mask
    )
    left_tile = left_tile.astype(jnp.bfloat16).transpose(2, 1, 0)
    right_tile = right_tile.astype(jnp.bfloat16).transpose(2, 1, 0)
    gate_term = jax.nn.sigmoid(projected[:, :, 4 * hidden :])
    right = swap(right_tile)
    left = swap(left_tile)
    right = lax.all_gather(right, "core", axis=0, tiled=False)
    right = right.reshape(2, 4, -1, rows_here)
    left = left.reshape(4, -1, rows_here)
    triangle = jnp.einsum(
        "czkj,bki->bzcji", right, left, preferred_element_type=jnp.float32
    ).astype(jnp.bfloat16)
    triangle = swap(triangle.reshape(hidden, cols_here, rows_here))
    normed_out = layer_norm(
        triangle.astype(jnp.float32), out_gain[:, None, None], out_bias[:, None, None], 0
    ).astype(jnp.bfloat16)
    out_proj = jnp.einsum("hji,hc->ijc", normed_out, out_weight, preferred_element_type=jnp.float32)
    return (gate_term * out_proj).astype(jnp.bfloat16)


def solution(mesh):
    fine = Mesh(mesh.devices.reshape(4, 2, 4, 2, 4), ("zl", "core", "x", "zh", "y"))
    tile = P(("zl", "core"), ("x", "zh", "y"), None)
    placed = (tile, P(), P(), P(), P(), P(), P(), P(), P())
    return jax.shard_map(local, mesh=fine, in_specs=placed, out_specs=tile, check_vma=False)
```

```python
import functools

import jax
import jax.numpy as jnp
from jax import lax
from jax.experimental import pallas as pl
from jax.experimental.pallas import tpu as pltpu
from jax.sharding import Mesh
from jax.sharding import PartitionSpec as P

CHIPS = ("x", "zl", "y", "zh")
VMEM_LIMIT = 40 * 1024 * 1024


def normalise(values, gain_row, bias_row):
    average = jnp.mean(values, axis=-1, keepdims=True)
    centred = values - average
    spread = jnp.mean(centred * centred, axis=-1, keepdims=True)
    return centred * lax.rsqrt(spread + 1e-05) * gain_row + bias_row


def contract(lhs, rhs, lhs_dim, rhs_dim):
    return lax.dot_general(
        lhs, rhs, (((lhs_dim,), (rhs_dim,)), ((), ())), preferred_element_type=jnp.float32
    )


def factors_kernel(
    row_index, col_index, mask_ref, mask_row_ref, x_ref, gain_ref, bias_ref, w_ref, out_ref, xn_ref, xs, ls, rs
):
    rows, part, channels = x_ref.shape
    hidden = w_ref.shape[2]
    step = pl.program_id(0)
    for first in range(0, rows, 16):
        piece = x_ref[first : first + 16].astype(jnp.float32).reshape(16 * part, channels)
        normed = normalise(piece, gain_ref[...], bias_ref[...])
        rounded = normed.astype(jnp.bfloat16)
        xn_ref[first : first + 16] = rounded.reshape(16, part, channels)
        xs[first * part : (first + 16) * part, :] = rounded.astype(jnp.float32)
    weights = jnp.concatenate([w_ref[n].T for n in range(4)], axis=0)
    row_mask = mask_row_ref[pl.ds(row_index(), 1), :].astype(jnp.float32)
    first_col = col_index() * (part * pl.num_programs(0)) + step * part
    for k in range(part):
        of_k = xs[pl.ds(k, rows, stride=part), :].astype(jnp.bfloat16)
        projected = contract(weights, of_k, 1, 1)
        mask = row_mask * mask_ref[first_col + k].astype(jnp.float32)
        left = jax.nn.sigmoid(projected[:hidden]) * projected[hidden : 2 * hidden] * mask
        right = (
            jax.nn.sigmoid(projected[2 * hidden : 3 * hidden]) * projected[3 * hidden :] * mask
        )
        ls[pl.ds(k, hidden, stride=part), :] = left
        rs[pl.ds(k, hidden, stride=part), :] = right
    out_ref[:, 0] = ls[...].reshape(hidden, part, rows).astype(jnp.bfloat16)
    out_ref[:, 1] = rs[...].reshape(hidden, part, rows).astype(jnp.bfloat16)


def row_of():
    return lax.axis_index("zl") * 2 + lax.axis_index("core")


def col_of():
    return (lax.axis_index("x") * 2 + lax.axis_index("zh")) * 4 + lax.axis_index("y")


def factors(pair_rep, residue_mask, in_gain, in_bias, in_weights, row=row_of, col=col_of):
    rows, cols, channels = pair_rep.shape
    hidden = in_weights.shape[2]
    part = 16
    whole = pl.BlockSpec(memory_space=pltpu.VMEM)
    return pl.pallas_call(
        functools.partial(factors_kernel, row, col),
        grid=(cols // part,),
        in_specs=[
            pl.BlockSpec(memory_space=pltpu.SMEM),
            whole,
            pl.BlockSpec((rows, part, channels), lambda s: (0, s, 0)),
            whole,
            whole,
            whole,
        ],
        out_specs=[
            pl.BlockSpec((hidden, 2, part, rows), lambda s: (0, 0, s, 0)),
            pl.BlockSpec((rows, part, channels), lambda s: (0, s, 0)),
        ],
        out_shape=[
            jax.ShapeDtypeStruct((hidden, 2, cols, rows), jnp.bfloat16),
            jax.ShapeDtypeStruct((rows, cols, channels), jnp.bfloat16),
        ],
        scratch_shapes=[
            pltpu.VMEM((rows * part, channels), jnp.float32),
            pltpu.VMEM((hidden * part, rows), jnp.float32),
            pltpu.VMEM((hidden * part, rows), jnp.float32),
        ],
        compiler_params=pltpu.CompilerParams(vmem_limit_bytes=VMEM_LIMIT),
        name="factors",
    )(
        residue_mask,
        residue_mask.reshape(-1, rows),
        pair_rep,
        in_gain.reshape(1, channels),
        in_bias.reshape(1, channels),
        in_weights,
    )


def gate_kernel(x_ref, w_ref, out_ref):
    rows, part, channels = x_ref.shape
    out_ref[...] = jax.nn.sigmoid(
        contract(x_ref[...].reshape(rows * part, channels), w_ref[...], 1, 0)
    ).reshape(rows, part, channels)


def gates(normed_in, gate_weight):
    rows, cols, channels = normed_in.shape
    part = 16
    return pl.pallas_call(
        gate_kernel,
        grid=(rows // part,),
        in_specs=[
            pl.BlockSpec((part, cols, channels), lambda s: (s, 0, 0)),
            pl.BlockSpec(memory_space=pltpu.VMEM),
        ],
        out_specs=pl.BlockSpec((part, cols, channels), lambda s: (s, 0, 0)),
        out_shape=jax.ShapeDtypeStruct((rows, cols, channels), jnp.float32),
        compiler_params=pltpu.CompilerParams(vmem_limit_bytes=VMEM_LIMIT),
        cost_estimate=pl.CostEstimate(
            flops=2 * rows * cols * channels * channels,
            bytes_accessed=6 * rows * cols * channels,
            transcendentals=rows * cols * channels,
        ),
        name="gates",
    )(normed_in, gate_weight)


def product_kernel(core_index, own, left_ref, right_ref, *refs):
    out_ref = refs[-1]
    many_x, many_z = left_ref.shape[:2]
    depth = left_ref.shape[2] * left_ref.shape[3] * left_ref.shape[4]
    wide = left_ref.shape[5]
    core = core_index()
    place = core if own else 1 - core
    for zj in range(many_z):
        rights = jnp.concatenate(
            [right_ref[x, zj].reshape(depth, wide) for x in range(many_x)], axis=0
        )
        lefts = jnp.concatenate(
            [
                jnp.concatenate(
                    [left_ref[x, zi].reshape(depth, wide) for x in range(many_x)], axis=0
                )
                for zi in range(many_z)
            ],
            axis=1,
        )
        out = contract(rights, lefts, 0, 0).astype(jnp.bfloat16)
        for zi in range(many_z):
            out_ref[zj, zi, :, place] = out[:, zi * wide : (zi + 1) * wide].reshape(
                4, wide // 4, wide
            )


def core_of():
    return lax.axis_index("core")


def product(left, right, own, before=None, core=core_of):
    many_x, many_z, many_y, many_h, cols, rows = left.shape
    whole = pl.BlockSpec(memory_space=pltpu.VMEM)
    given = [left, right] if before is None else [left, right, before]
    specs = [whole, whole] if before is None else [whole, whole, pl.BlockSpec(memory_space=pl.ANY)]
    return pl.pallas_call(
        functools.partial(product_kernel, core, own),
        in_specs=specs,
        out_specs=whole,
        out_shape=jax.ShapeDtypeStruct(left.shape, jnp.bfloat16),
        compiler_params=pltpu.CompilerParams(vmem_limit_bytes=VMEM_LIMIT),
        name="product",
    )(*given)


def finish_kernel(t_ref, gate_ref, gain_ref, bias_ref, w_ref, out_ref, ts, os):
    hidden, part, rows = t_ref.shape
    channels = w_ref.shape[1]
    values = t_ref[...].astype(jnp.float32)
    ts[...] = values.reshape(hidden * part, rows)
    average = jnp.sum(values, axis=0) * (1.0 / hidden)
    centred = values - average[None]
    spread = jnp.sum(centred * centred, axis=0) * (1.0 / hidden)
    scale = lax.rsqrt(spread + 1e-05)
    gain = jnp.broadcast_to(gain_ref[...], (hidden, rows))
    bias = jnp.broadcast_to(bias_ref[...], (hidden, rows))
    for j in range(part):
        of_j = ts[pl.ds(j, hidden, stride=part), :]
        normed = (of_j - average[j : j + 1]) * scale[j : j + 1] * gain + bias
        os[pl.ds(j, rows, stride=part), :] = contract(
            normed.astype(jnp.bfloat16), w_ref[...], 0, 0
        )
    out_ref[...] = (os[...].reshape(rows, part, channels) * gate_ref[...]).astype(jnp.bfloat16)


def finish(triangle, gate, out_gain, out_bias, out_weight):
    hidden, cols, rows = triangle.shape
    channels = out_weight.shape[1]
    part = 16
    whole = pl.BlockSpec(memory_space=pltpu.VMEM)
    return pl.pallas_call(
        finish_kernel,
        grid=(cols // part,),
        in_specs=[
            pl.BlockSpec((hidden, part, rows), lambda s: (0, s, 0)),
            pl.BlockSpec((rows, part, channels), lambda s: (0, s, 0)),
            whole,
            whole,
            whole,
        ],
        out_specs=pl.BlockSpec((rows, part, channels), lambda s: (0, s, 0)),
        out_shape=jax.ShapeDtypeStruct((rows, cols, channels), jnp.bfloat16),
        scratch_shapes=[
            pltpu.VMEM((hidden * part, rows), jnp.float32),
            pltpu.VMEM((rows * part, channels), jnp.float32),
        ],
        compiler_params=pltpu.CompilerParams(vmem_limit_bytes=VMEM_LIMIT),
        name="finish",
    )(
        triangle,
        gate,
        out_gain.reshape(hidden, 1),
        out_bias.reshape(hidden, 1),
        out_weight,
    )


def swap(chunks):
    return lax.all_to_all(chunks, CHIPS, split_axis=0, concat_axis=0, tiled=True)


def local(
    pair_rep,
    residue_mask,
    in_gain,
    in_bias,
    in_weights,
    gate_weight,
    out_gain,
    out_bias,
    out_weight,
):
    rows, cols, channels = pair_rep.shape
    hidden = in_weights.shape[2]
    both, normed_in = factors(pair_rep, residue_mask, in_gain, in_bias, in_weights)
    both = swap(both.reshape(hidden, 2 * cols, rows))
    gate = gates(normed_in, gate_weight)
    both = both.reshape(4, 4, 4, 2, 2, cols, rows)
    left, right = both[:, :, :, :, 0], both[:, :, :, :, 1]
    other = lax.ppermute(right, "core", [(0, 1), (1, 0)])
    core = lax.axis_index("core")
    rights = jnp.where(core == 0, jnp.stack([right, other]), jnp.stack([other, right]))
    triangle = jnp.einsum(
        "cxzyhkj,xwyhki->zwcji", rights, left, preferred_element_type=jnp.float32
    ).astype(jnp.bfloat16)
    triangle = triangle.reshape(4, 4, 2, 4, cols, rows).transpose(0, 1, 3, 2, 4, 5)
    triangle = swap(triangle.reshape(hidden, cols, rows))
    return finish(triangle, gate, out_gain, out_bias, out_weight)


def solution(mesh):
    fine = Mesh(mesh.devices.reshape(4, 2, 4, 2, 4), ("zl", "core", "x", "zh", "y"))
    tile = P(("zl", "core"), ("x", "zh", "y"), None)
    placed = (tile, P(), P(), P(), P(), P(), P(), P(), P())
    return jax.shard_map(local, mesh=fine, in_specs=placed, out_specs=tile, check_vma=False)
```

```python
import functools

import jax
import jax.numpy as jnp
from jax import lax
from jax.experimental import pallas as pl
from jax.experimental.pallas import tpu as pltpu
from jax.sharding import Mesh
from jax.sharding import PartitionSpec as P

AXES = ("zl", "core", "x", "zh", "y")
ORDER = ("y0", "z0", "x0", "z2", "y1", "x1", "z1")
VMEM_LIMIT = 60 * 1024 * 1024


def chips():
    places = []
    for place in range(1 << len(ORDER)):
        at = {"z": 0, "x": 0, "y": 0}
        for n, (axis, bit) in enumerate(ORDER):
            at[axis] |= ((place >> (len(ORDER) - 1 - n)) & 1) << int(bit)
        places.append((at["z"], at["x"], at["y"]))
    return places


CHIPS = chips()
PLACE = {chip: place for place, chip in enumerate(CHIPS)}
GROUPS = [
    [(((z % 4 * 2 + core) * 4 + x) * 2 + z // 4) * 4 + y for z, x, y in CHIPS] for core in range(2)
]


def contract(lhs, rhs, lhs_dim, rhs_dim):
    return lax.dot_general(
        lhs, rhs, (((lhs_dim,), (rhs_dim,)), ((), ())), preferred_element_type=jnp.float32
    )


def gated(gate, value):
    return value * pltpu.reciprocal(1.0 + jnp.exp(-gate), approx=True)


def normalise(values, gain_row, bias_row):
    average = jnp.mean(values, axis=-1, keepdims=True)
    centred = values - average
    spread = jnp.mean(centred * centred, axis=-1, keepdims=True)
    return centred * lax.rsqrt(spread + 1e-05) * gain_row + bias_row


def factors_kernel(
    row_index, col_index, mask_ref, mask_row_ref, x_ref, gain_ref, bias_ref, w_ref, out_ref, xn_ref, xs, ls, rs
):
    rows, part, channels = x_ref.shape
    hidden = w_ref.shape[2]
    step = pl.program_id(0)
    for first in range(0, rows, 16):
        piece = x_ref[first : first + 16].astype(jnp.float32).reshape(16 * part, channels)
        normed = normalise(piece, gain_ref[...], bias_ref[...])
        xn_ref[first : first + 16] = normed.astype(jnp.bfloat16).reshape(16, part, channels)
        xs[first * part : (first + 16) * part, :] = normed
    weights = jnp.concatenate([w_ref[n].T for n in range(4)], axis=0)
    row_mask = mask_row_ref[pl.ds(row_index(), 1), :].astype(jnp.float32)
    first_col = col_index() * (part * pl.num_programs(0)) + step * part
    for k in range(part):
        of_k = xs[pl.ds(k, rows, stride=part), :].astype(jnp.bfloat16)
        projected = contract(weights, of_k, 1, 1)
        mask = row_mask * mask_ref[first_col + k].astype(jnp.float32)
        ls[pl.ds(k, hidden, stride=part), :] = (
            gated(projected[:hidden], projected[hidden : 2 * hidden]) * mask
        )
        rs[pl.ds(k, hidden, stride=part), :] = (
            gated(projected[2 * hidden : 3 * hidden], projected[3 * hidden :]) * mask
        )
    out_ref[:, 0] = ls[...].reshape(hidden, part, rows).astype(jnp.bfloat16)
    out_ref[:, 1] = rs[...].reshape(hidden, part, rows).astype(jnp.bfloat16)


def row_of():
    return lax.axis_index("zl") * 2 + lax.axis_index("core")


def col_of():
    return (lax.axis_index("x") * 2 + lax.axis_index("zh")) * 4 + lax.axis_index("y")


def core_of():
    return lax.axis_index("core")


def fixed(shape):
    return pl.BlockSpec(shape, lambda s: (0,) * len(shape))


def factors(pair_rep, residue_mask, in_gain, in_bias, in_weights, row=row_of, col=col_of):
    rows, cols, channels = pair_rep.shape
    hidden = in_weights.shape[2]
    part = 16
    return pl.pallas_call(
        functools.partial(factors_kernel, row, col),
        grid=(cols // part,),
        in_specs=[
            pl.BlockSpec(memory_space=pltpu.SMEM),
            fixed((residue_mask.shape[0] // rows, rows)),
            pl.BlockSpec((rows, part, channels), lambda s: (0, s, 0)),
            fixed((1, channels)),
            fixed((1, channels)),
            fixed(in_weights.shape),
        ],
        out_specs=[
            pl.BlockSpec((hidden, 2, part, rows), lambda s: (0, 0, s, 0)),
            pl.BlockSpec((rows, part, channels), lambda s: (0, s, 0)),
        ],
        out_shape=[
            jax.ShapeDtypeStruct((hidden, 2, cols, rows), jnp.bfloat16),
            jax.ShapeDtypeStruct((rows, cols, channels), jnp.bfloat16),
        ],
        scratch_shapes=[
            pltpu.VMEM((rows * part, channels), jnp.float32),
            pltpu.VMEM((hidden * part, rows), jnp.float32),
            pltpu.VMEM((hidden * part, rows), jnp.float32),
        ],
        compiler_params=pltpu.CompilerParams(vmem_limit_bytes=VMEM_LIMIT),
        name="factors",
    )(
        residue_mask,
        residue_mask.reshape(-1, rows),
        pair_rep,
        in_gain.reshape(1, channels),
        in_bias.reshape(1, channels),
        in_weights,
    )


def gate_kernel(x_ref, w_ref, out_ref):
    rows, part, channels = x_ref.shape
    out_ref[...] = gated(
        contract(x_ref[...].reshape(rows * part, channels), w_ref[...], 1, 0), 1.0
    ).reshape(rows, part, channels)


def gates(normed_in, gate_weight):
    rows, cols, channels = normed_in.shape
    part = 32
    return pl.pallas_call(
        gate_kernel,
        grid=(rows // part,),
        in_specs=[
            pl.BlockSpec((part, cols, channels), lambda s: (s, 0, 0)),
            fixed(gate_weight.shape),
        ],
        out_specs=pl.BlockSpec((part, cols, channels), lambda s: (s, 0, 0)),
        out_shape=jax.ShapeDtypeStruct((rows, cols, channels), jnp.float32),
        compiler_params=pltpu.CompilerParams(vmem_limit_bytes=16 * 1024 * 1024),
        cost_estimate=pl.CostEstimate(
            flops=2 * rows * cols * channels * channels,
            bytes_accessed=6 * rows * cols * channels,
            transcendentals=rows * cols * channels,
        ),
        name="gates",
    )(normed_in, gate_weight)


def blocks(ref, which, zl):
    return jnp.concatenate(
        [
            ref[PLACE[zl + 4 * zh, x, y], which] if which is not None else ref[PLACE[zl + 4 * zh, x, y]]
            for x in range(4)
            for zh in range(2)
            for y in range(4)
        ],
        axis=0,
    )


def half_kernel(both_ref, out_ref):
    lefts = jnp.concatenate([blocks(both_ref, 0, zl) for zl in range(4)], axis=1)
    rights = jnp.concatenate([blocks(both_ref, 1, zl) for zl in range(4)], axis=1)
    out_ref[...] = contract(rights, lefts, 0, 0).astype(jnp.bfloat16)


def product_kernel(core_index, both_ref, right_ref, half_ref, out_ref):
    cols, wide = right_ref.shape[1:]
    core = core_index()
    lefts = jnp.concatenate([blocks(both_ref, 0, zl) for zl in range(4)], axis=1)
    rights = jnp.concatenate([blocks(right_ref, None, zl) for zl in range(4)], axis=1)
    out = contract(rights, lefts, 0, 0).astype(jnp.bfloat16)
    for zl in range(4):
        for x in range(4):
            for y in range(4):
                low, high = PLACE[zl, x, y], PLACE[zl + 4, x, y]
                place = (pl.ds(x * wide + y * cols, cols), pl.ds(zl * wide, wide))
                out_ref[low + core * (high - low)] = half_ref[place]
                out_ref[high + core * (low - high)] = out[
                    x * wide + y * cols : x * wide + (y + 1) * cols, zl * wide : (zl + 1) * wide
                ]


def half(both):
    rows = both.shape[3]
    whole = pl.BlockSpec(memory_space=pltpu.VMEM)
    return pl.pallas_call(
        half_kernel,
        in_specs=[whole],
        out_specs=whole,
        out_shape=jax.ShapeDtypeStruct((4 * rows, 4 * rows), jnp.bfloat16),
        compiler_params=pltpu.CompilerParams(vmem_limit_bytes=24 * 1024 * 1024),
        cost_estimate=pl.CostEstimate(
            flops=2 * 512 * 512 * 1024, bytes_accessed=5 << 19, transcendentals=0
        ),
        name="half",
    )(both)


def product(both, right, own, core=core_of):
    whole = pl.BlockSpec(memory_space=pltpu.VMEM)
    return pl.pallas_call(
        functools.partial(product_kernel, core),
        in_specs=[whole, whole, whole],
        out_specs=whole,
        out_shape=jax.ShapeDtypeStruct(right.shape, jnp.bfloat16),
        compiler_params=pltpu.CompilerParams(vmem_limit_bytes=24 * 1024 * 1024),
        name="product",
    )(both, right, own)


def finish_kernel(t_ref, gate_ref, gain_ref, bias_ref, w_ref, out_ref, ts, os):
    hidden, part, rows = t_ref.shape
    channels = w_ref.shape[1]
    values = t_ref[...].astype(jnp.float32)
    ts[...] = values.reshape(hidden * part, rows)
    average = jnp.sum(values, axis=0) * (1.0 / hidden)
    centred = values - average[None]
    spread = jnp.sum(centred * centred, axis=0) * (1.0 / hidden)
    scale = lax.rsqrt(spread + 1e-05)
    gain = jnp.broadcast_to(gain_ref[...], (hidden, rows))
    bias = jnp.broadcast_to(bias_ref[...], (hidden, rows))
    for j in range(part):
        of_j = ts[pl.ds(j, hidden, stride=part), :]
        normed = (of_j - average[j : j + 1]) * scale[j : j + 1] * gain + bias
        os[pl.ds(j, rows, stride=part), :] = contract(
            normed.astype(jnp.bfloat16), w_ref[...], 0, 0
        )
    out_ref[...] = (os[...].reshape(rows, part, channels) * gate_ref[...]).astype(jnp.bfloat16)


def finish(triangle, gate, out_gain, out_bias, out_weight):
    hidden, cols, rows = triangle.shape
    channels = out_weight.shape[1]
    part = 16
    whole = pl.BlockSpec(memory_space=pltpu.VMEM)
    return pl.pallas_call(
        finish_kernel,
        grid=(cols // part,),
        in_specs=[
            pl.BlockSpec((hidden, part, rows), lambda s: (0, s, 0)),
            pl.BlockSpec((rows, part, channels), lambda s: (0, s, 0)),
            whole,
            whole,
            whole,
        ],
        out_specs=pl.BlockSpec((rows, part, channels), lambda s: (0, s, 0)),
        out_shape=jax.ShapeDtypeStruct((rows, cols, channels), jnp.bfloat16),
        scratch_shapes=[
            pltpu.VMEM((hidden * part, rows), jnp.float32),
            pltpu.VMEM((rows * part, channels), jnp.float32),
        ],
        compiler_params=pltpu.CompilerParams(vmem_limit_bytes=32 * 1024 * 1024),
        name="finish",
    )(
        triangle,
        gate,
        out_gain.reshape(hidden, 1),
        out_bias.reshape(hidden, 1),
        out_weight,
    )


def swap(chunks):
    return lax.all_to_all(
        chunks, AXES, split_axis=0, concat_axis=0, tiled=True, axis_index_groups=GROUPS
    )


def local(
    pair_rep,
    residue_mask,
    in_gain,
    in_bias,
    in_weights,
    gate_weight,
    out_gain,
    out_bias,
    out_weight,
):
    rows, cols, channels = pair_rep.shape
    hidden = in_weights.shape[2]
    both, normed_in = factors(pair_rep, residue_mask, in_gain, in_bias, in_weights)
    both = swap(both.reshape(hidden, 2 * cols, rows)).reshape(hidden, 2, cols, rows)
    right, normed_in = lax.optimization_barrier((both[:, 1], normed_in))
    other = lax.ppermute(right, "core", [(0, 1), (1, 0)])
    own = half(both)
    gate = gates(normed_in, gate_weight)
    other, own, gate = lax.optimization_barrier((other, own, gate))
    triangle = swap(product(both, other, own))
    return finish(triangle, gate, out_gain, out_bias, out_weight)


def solution(mesh):
    fine = Mesh(mesh.devices.reshape(4, 2, 4, 2, 4), AXES)
    tile = P(("zl", "core"), ("x", "zh", "y"), None)
    placed = (tile, P(), P(), P(), P(), P(), P(), P(), P())
    return jax.shard_map(local, mesh=fine, in_specs=placed, out_specs=tile, check_vma=False)
```

```python
import functools

import jax
import jax.numpy as jnp
from jax import lax
from jax.experimental import pallas as pl
from jax.experimental.pallas import tpu as pltpu
from jax.sharding import Mesh
from jax.sharding import PartitionSpec as P

AXES = ("zl", "core", "x", "zh", "y")
ORDER = ("y0", "z0", "x0", "z2", "y1", "x1", "z1")
VMEM_LIMIT = 60 * 1024 * 1024
APART = 17


def chips():
    places = []
    for place in range(1 << len(ORDER)):
        at = {"z": 0, "x": 0, "y": 0}
        for n, (axis, bit) in enumerate(ORDER):
            at[axis] |= ((place >> (len(ORDER) - 1 - n)) & 1) << int(bit)
        places.append((at["z"], at["x"], at["y"]))
    return places


CHIPS = chips()
PLACE = {chip: place for place, chip in enumerate(CHIPS)}
GROUPS = [
    [(((z % 4 * 2 + core) * 4 + x) * 2 + z // 4) * 4 + y for z, x, y in CHIPS] for core in range(2)
]


def contract(lhs, rhs, lhs_dim, rhs_dim):
    return lax.dot_general(
        lhs, rhs, (((lhs_dim,), (rhs_dim,)), ((), ())), preferred_element_type=jnp.float32
    )


def gated(gate, value):
    return value * pltpu.reciprocal(1.0 + jnp.exp(-gate), approx=True)


def normalise(values, gain_row, bias_row):
    average = jnp.mean(values, axis=-1, keepdims=True)
    centred = values - average
    spread = jnp.mean(centred * centred, axis=-1, keepdims=True)
    return centred * lax.rsqrt(spread + 1e-05) * gain_row + bias_row


def factors_kernel(
    row_index, col_index, mask_ref, mask_row_ref, x_hbm, gain_ref, bias_ref, w_hbm, out_hbm, x_ref, w_ref, out_ref, xs, ls, rs, sems
):
    rows, cols, channels = x_hbm.shape
    hidden = w_hbm.shape[2]
    part = 16
    parts = cols // part
    copies = [
        pltpu.make_async_copy(
            x_hbm.at[:, pl.ds(n * part, part)], x_ref.at[n], sems.at[n]
        )
        for n in range(parts)
    ]
    load_w = pltpu.make_async_copy(w_hbm, w_ref, sems.at[parts])
    load_w.start()
    for copy in copies:
        copy.start()
    load_w.wait()
    weights = jnp.concatenate([w_ref[m].T for m in range(4)], axis=0)
    stores = []
    row_mask = mask_row_ref[pl.ds(row_index(), 1), :].astype(jnp.float32)
    first_col = col_index() * cols
    for n in range(parts):
        copies[n].wait()
        for first in range(0, rows, 16):
            piece = x_ref[n, first : first + 16].astype(jnp.float32).reshape(16 * part, channels)
            normed = normalise(piece, gain_ref[...], bias_ref[...])
            for i in range(16):
                xs[(first + i) * APART : (first + i) * APART + part, :] = normed[i * part : (i + 1) * part]
        for k in range(0, part, 2):
            of_k = jnp.concatenate(
                [xs[pl.ds(k + d, rows, stride=APART), :].astype(jnp.bfloat16) for d in range(2)],
                axis=0,
            )
            projected = contract(weights, of_k, 1, 1)
            for d in range(2):
                mine = projected[:, d * rows : (d + 1) * rows]
                mask = row_mask * mask_ref[first_col + n * part + k + d].astype(jnp.float32)
                ls[pl.ds(k + d, hidden, stride=APART), :] = (
                    gated(mine[:hidden], mine[hidden : 2 * hidden]) * mask
                )
                rs[pl.ds(k + d, hidden, stride=APART), :] = (
                    gated(mine[2 * hidden : 3 * hidden], mine[3 * hidden :]) * mask
                )
        here = slice(n * part, (n + 1) * part)
        for h in range(hidden):
            out_ref[h, 0, here] = ls[h * APART : h * APART + part].astype(jnp.bfloat16)
            out_ref[h, 1, here] = rs[h * APART : h * APART + part].astype(jnp.bfloat16)
        stores.append(
            pltpu.make_async_copy(
                out_ref.at[:, :, pl.ds(n * part, part)],
                out_hbm.at[:, :, pl.ds(n * part, part)],
                sems.at[parts + 1 + n],
            )
        )
        stores[-1].start()
    for store in stores:
        store.wait()


def row_of():
    return lax.axis_index("zl") * 2 + lax.axis_index("core")


def col_of():
    return (lax.axis_index("x") * 2 + lax.axis_index("zh")) * 4 + lax.axis_index("y")


def core_of():
    return lax.axis_index("core")


def fixed(shape):
    return pl.BlockSpec(shape, lambda s: (0,) * len(shape))


def factors(pair_rep, residue_mask, in_gain, in_bias, in_weights, row=row_of, col=col_of):
    rows, cols, channels = pair_rep.shape
    hidden = in_weights.shape[2]
    part = 16
    whole = pl.BlockSpec(memory_space=pltpu.VMEM)
    far = pl.BlockSpec(memory_space=pltpu.HBM)
    return pl.pallas_call(
        functools.partial(factors_kernel, row, col),
        in_specs=[pl.BlockSpec(memory_space=pltpu.SMEM), whole, far, whole, whole, far],
        out_specs=far,
        out_shape=jax.ShapeDtypeStruct((hidden, 2, cols, rows), jnp.bfloat16),
        scratch_shapes=[
            pltpu.VMEM((cols // part, rows, part, channels), jnp.bfloat16),
            pltpu.VMEM(in_weights.shape, jnp.bfloat16),
            pltpu.VMEM((hidden, 2, cols, rows), jnp.bfloat16),
            pltpu.VMEM((rows * APART, channels), jnp.float32),
            pltpu.VMEM((hidden * APART, rows), jnp.float32),
            pltpu.VMEM((hidden * APART, rows), jnp.float32),
            pltpu.SemaphoreType.DMA((2 * (cols // part) + 1,)),
        ],
        compiler_params=pltpu.CompilerParams(vmem_limit_bytes=VMEM_LIMIT),
        name="factors",
    )(
        residue_mask,
        residue_mask.reshape(-1, rows),
        pair_rep,
        in_gain.reshape(1, channels),
        in_bias.reshape(1, channels),
        in_weights,
    )


def gate_kernel(x_ref, gain_ref, bias_ref, w_ref, out_ref):
    rows, cols, channels = x_ref.shape
    values = x_ref[...].astype(jnp.float32).reshape(rows * cols, channels)
    normed = normalise(values, gain_ref[...], bias_ref[...]).astype(jnp.bfloat16)
    out_ref[...] = gated(contract(normed, w_ref[...], 1, 0), 1.0).reshape(rows, cols, channels)


def gates(pair_rep, in_gain, in_bias, gate_weight):
    rows, cols, channels = pair_rep.shape
    part = 16
    block = pl.BlockSpec((part, cols, channels), lambda s: (s, 0, 0))
    return pl.pallas_call(
        gate_kernel,
        grid=(rows // part,),
        in_specs=[block, fixed((1, channels)), fixed((1, channels)), fixed(gate_weight.shape)],
        out_specs=block,
        out_shape=jax.ShapeDtypeStruct((rows, cols, channels), jnp.float32),
        compiler_params=pltpu.CompilerParams(vmem_limit_bytes=16 * 1024 * 1024),
        cost_estimate=pl.CostEstimate(
            flops=2 * rows * cols * channels * channels,
            bytes_accessed=6 * rows * cols * channels,
            transcendentals=rows * cols * channels,
        ),
        name="gates",
    )(pair_rep, in_gain.reshape(1, channels), in_bias.reshape(1, channels), gate_weight)


def blocks(ref, which, zl):
    return jnp.concatenate(
        [
            ref[PLACE[zl + 4 * zh, x, y], which] if which is not None else ref[PLACE[zl + 4 * zh, x, y]]
            for x in range(4)
            for zh in range(2)
            for y in range(4)
        ],
        axis=0,
    )


def half_kernel(both_ref, out_ref):
    lefts = jnp.concatenate([blocks(both_ref, 0, zl) for zl in range(4)], axis=1)
    rights = jnp.concatenate([blocks(both_ref, 1, zl) for zl in range(4)], axis=1)
    out_ref[...] = contract(rights, lefts, 0, 0).astype(jnp.bfloat16)


def product_kernel(core_index, both_ref, right_ref, half_ref, out_ref):
    cols, wide = right_ref.shape[1:]
    core = core_index()
    lefts = jnp.concatenate([blocks(both_ref, 0, zl) for zl in range(4)], axis=1)
    rights = jnp.concatenate([blocks(right_ref, None, zl) for zl in range(4)], axis=1)
    out = contract(rights, lefts, 0, 0).astype(jnp.bfloat16)
    for zl in range(4):
        for x in range(4):
            for y in range(4):
                low, high = PLACE[zl, x, y], PLACE[zl + 4, x, y]
                place = (pl.ds(x * wide + y * cols, cols), pl.ds(zl * wide, wide))
                out_ref[low + core * (high - low)] = half_ref[place]
                out_ref[high + core * (low - high)] = out[
                    x * wide + y * cols : x * wide + (y + 1) * cols, zl * wide : (zl + 1) * wide
                ]


def half(both):
    rows = both.shape[3]
    whole = pl.BlockSpec(memory_space=pltpu.VMEM)
    return pl.pallas_call(
        half_kernel,
        in_specs=[whole],
        out_specs=whole,
        out_shape=jax.ShapeDtypeStruct((4 * rows, 4 * rows), jnp.bfloat16),
        compiler_params=pltpu.CompilerParams(vmem_limit_bytes=24 * 1024 * 1024),
        cost_estimate=pl.CostEstimate(
            flops=2 * 512 * 512 * 1024, bytes_accessed=5 << 19, transcendentals=0
        ),
        name="half",
    )(both)


def product(both, right, own, core=core_of):
    whole = pl.BlockSpec(memory_space=pltpu.VMEM)
    return pl.pallas_call(
        functools.partial(product_kernel, core),
        in_specs=[whole, whole, whole],
        out_specs=whole,
        out_shape=jax.ShapeDtypeStruct(right.shape, jnp.bfloat16),
        compiler_params=pltpu.CompilerParams(vmem_limit_bytes=24 * 1024 * 1024),
        name="product",
    )(both, right, own)


def finish_kernel(t_ref, gate_ref, gain_ref, bias_ref, w_ref, out_ref, ts, os):
    hidden, part, rows = t_ref.shape
    channels = w_ref.shape[1]
    values = t_ref[...].astype(jnp.float32)
    for h in range(hidden):
        ts[h * APART : h * APART + part, :] = values[h]
    average = jnp.sum(values, axis=0) * (1.0 / hidden)
    centred = values - average[None]
    spread = jnp.sum(centred * centred, axis=0) * (1.0 / hidden)
    scale = lax.rsqrt(spread + 1e-05)
    gain = jnp.broadcast_to(gain_ref[...], (rows, hidden)).T
    bias = jnp.broadcast_to(bias_ref[...], (rows, hidden)).T
    for j in range(part):
        of_j = ts[pl.ds(j, hidden, stride=APART), :]
        normed = (of_j - average[j : j + 1]) * scale[j : j + 1] * gain + bias
        os[pl.ds(j, rows, stride=APART), :] = contract(
            normed.astype(jnp.bfloat16), w_ref[...], 0, 0
        )
    for i in range(rows):
        out_ref[i] = (os[i * APART : i * APART + part, :] * gate_ref[i]).astype(jnp.bfloat16)


def finish(triangle, gate, out_gain, out_bias, out_weight):
    hidden, cols, rows = triangle.shape
    channels = out_weight.shape[1]
    part = 16
    whole = pl.BlockSpec(memory_space=pltpu.VMEM)
    return pl.pallas_call(
        finish_kernel,
        grid=(cols // part,),
        in_specs=[
            pl.BlockSpec((hidden, part, rows), lambda s: (0, s, 0)),
            pl.BlockSpec((rows, part, channels), lambda s: (0, s, 0)),
            whole,
            whole,
            whole,
        ],
        out_specs=pl.BlockSpec((rows, part, channels), lambda s: (0, s, 0)),
        out_shape=jax.ShapeDtypeStruct((rows, cols, channels), jnp.bfloat16),
        scratch_shapes=[
            pltpu.VMEM((hidden * APART, rows), jnp.float32),
            pltpu.VMEM((rows * APART, channels), jnp.float32),
        ],
        compiler_params=pltpu.CompilerParams(vmem_limit_bytes=32 * 1024 * 1024),
        name="finish",
    )(
        triangle,
        gate,
        out_gain.reshape(1, hidden),
        out_bias.reshape(1, hidden),
        out_weight,
    )


def swap(chunks):
    return lax.all_to_all(
        chunks, AXES, split_axis=0, concat_axis=0, tiled=True, axis_index_groups=GROUPS
    )


def local(
    pair_rep,
    residue_mask,
    in_gain,
    in_bias,
    in_weights,
    gate_weight,
    out_gain,
    out_bias,
    out_weight,
):
    rows, cols, channels = pair_rep.shape
    hidden = in_weights.shape[2]
    both = factors(pair_rep, residue_mask, in_gain, in_bias, in_weights)
    both, late = lax.optimization_barrier((both, pair_rep))
    both = swap(both.reshape(hidden, 2 * cols, rows)).reshape(hidden, 2, cols, rows)
    gate = gates(late, in_gain, in_bias, gate_weight)
    both, gate = lax.optimization_barrier((both, gate))
    other = lax.ppermute(both[:, 1], "core", [(0, 1), (1, 0)])
    own = half(both)
    triangle = swap(product(both, other, own))
    return finish(triangle, gate, out_gain, out_bias, out_weight)


def solution(mesh):
    fine = Mesh(mesh.devices.reshape(4, 2, 4, 2, 4), AXES)
    tile = P(("zl", "core"), ("x", "zh", "y"), None)
    placed = (tile, P(), P(), P(), P(), P(), P(), P(), P())
    return jax.shard_map(local, mesh=fine, in_specs=placed, out_specs=tile, check_vma=False)
```

```python
import functools

import jax
import jax.numpy as jnp
from jax import lax
from jax.experimental import pallas as pl
from jax.experimental.pallas import tpu as pltpu
from jax.sharding import Mesh
from jax.sharding import PartitionSpec as P

AXES = ("zl", "core", "x", "zh", "y")
ORDER = ("z1", "x1", "y1", "z2", "z0", "x0", "y0")
VMEM_LIMIT = 60 * 1024 * 1024
APART = 17


def chips():
    places = []
    for place in range(1 << len(ORDER)):
        at = {"z": 0, "x": 0, "y": 0}
        for n, (axis, bit) in enumerate(ORDER):
            at[axis] |= ((place >> (len(ORDER) - 1 - n)) & 1) << int(bit)
        places.append((7 - at["z"], 3 - at["x"], 3 - at["y"]))
    return places


CHIPS = chips()
PLACE = {chip: place for place, chip in enumerate(CHIPS)}
GROUPS = [
    [(((z % 4 * 2 + core) * 4 + x) * 2 + z // 4) * 4 + y for z, x, y in CHIPS] for core in range(2)
]


def contract(lhs, rhs, lhs_dim, rhs_dim):
    return lax.dot_general(
        lhs, rhs, (((lhs_dim,), (rhs_dim,)), ((), ())), preferred_element_type=jnp.float32
    )


def gated(gate, value):
    return value * pltpu.reciprocal(1.0 + jnp.exp(-gate), approx=True)


def normalise(values, gain_row, bias_row):
    average = jnp.mean(values, axis=-1, keepdims=True)
    centred = values - average
    spread = jnp.mean(centred * centred, axis=-1, keepdims=True)
    return centred * lax.rsqrt(spread + 1e-05) * gain_row + bias_row


def factors_kernel(
    row_index, col_index, mask_ref, mask_row_ref, x_hbm, gain_ref, bias_ref, w_hbm, out_hbm, x_ref, w_ref, out_ref, xs, ls, rs, sems
):
    rows, cols, channels = x_hbm.shape
    hidden = w_hbm.shape[2]
    part = 16
    parts = cols // part
    copies = [
        pltpu.make_async_copy(
            x_hbm.at[:, pl.ds(n * part, part)], x_ref.at[n], sems.at[n]
        )
        for n in range(parts)
    ]
    load_w = pltpu.make_async_copy(w_hbm, w_ref, sems.at[parts])
    load_w.start()
    for copy in copies:
        copy.start()
    load_w.wait()
    weights = jnp.concatenate([w_ref[m].T for m in range(4)], axis=0)
    stores = []
    row_mask = mask_row_ref[pl.ds(row_index(), 1), :].astype(jnp.float32)
    first_col = col_index() * cols
    for n in range(parts):
        copies[n].wait()
        for first in range(0, rows, 16):
            piece = x_ref[n, first : first + 16].astype(jnp.float32).reshape(16 * part, channels)
            normed = normalise(piece, gain_ref[...], bias_ref[...])
            for i in range(16):
                xs[(first + i) * APART : (first + i) * APART + part, :] = normed[i * part : (i + 1) * part]
        for k in range(0, part, 2):
            of_k = jnp.concatenate(
                [xs[pl.ds(k + d, rows, stride=APART), :].astype(jnp.bfloat16) for d in range(2)],
                axis=0,
            )
            projected = contract(weights, of_k, 1, 1)
            for d in range(2):
                mine = projected[:, d * rows : (d + 1) * rows]
                mask = row_mask * mask_ref[first_col + n * part + k + d].astype(jnp.float32)
                ls[pl.ds(k + d, hidden, stride=APART), :] = (
                    gated(mine[:hidden], mine[hidden : 2 * hidden]) * mask
                )
                rs[pl.ds(k + d, hidden, stride=APART), :] = (
                    gated(mine[2 * hidden : 3 * hidden], mine[3 * hidden :]) * mask
                )
        here = slice(n * part, (n + 1) * part)
        for h in range(hidden):
            out_ref[h, 0, here] = ls[h * APART : h * APART + part].astype(jnp.bfloat16)
            out_ref[h, 1, here] = rs[h * APART : h * APART + part].astype(jnp.bfloat16)
        stores.append(
            pltpu.make_async_copy(
                out_ref.at[:, :, pl.ds(n * part, part)],
                out_hbm.at[:, :, pl.ds(n * part, part)],
                sems.at[parts + 1 + n],
            )
        )
        stores[-1].start()
    for store in stores:
        store.wait()


def row_of():
    return lax.axis_index("zl") * 2 + lax.axis_index("core")


def col_of():
    return (lax.axis_index("x") * 2 + lax.axis_index("zh")) * 4 + lax.axis_index("y")


def core_of():
    return lax.axis_index("core")


def fixed(shape):
    return pl.BlockSpec(shape, lambda s: (0,) * len(shape))


def factors(pair_rep, residue_mask, in_gain, in_bias, in_weights, row=row_of, col=col_of):
    rows, cols, channels = pair_rep.shape
    hidden = in_weights.shape[2]
    part = 16
    whole = pl.BlockSpec(memory_space=pltpu.VMEM)
    far = pl.BlockSpec(memory_space=pltpu.HBM)
    return pl.pallas_call(
        functools.partial(factors_kernel, row, col),
        in_specs=[pl.BlockSpec(memory_space=pltpu.SMEM), whole, far, whole, whole, far],
        out_specs=far,
        out_shape=jax.ShapeDtypeStruct((hidden, 2, cols, rows), jnp.bfloat16),
        scratch_shapes=[
            pltpu.VMEM((cols // part, rows, part, channels), jnp.bfloat16),
            pltpu.VMEM(in_weights.shape, jnp.bfloat16),
            pltpu.VMEM((hidden, 2, cols, rows), jnp.bfloat16),
            pltpu.VMEM((rows * APART, channels), jnp.float32),
            pltpu.VMEM((hidden * APART, rows), jnp.float32),
            pltpu.VMEM((hidden * APART, rows), jnp.float32),
            pltpu.SemaphoreType.DMA((2 * (cols // part) + 1,)),
        ],
        compiler_params=pltpu.CompilerParams(vmem_limit_bytes=VMEM_LIMIT),
        name="factors",
    )(
        residue_mask,
        residue_mask.reshape(-1, rows),
        pair_rep,
        in_gain.reshape(1, channels),
        in_bias.reshape(1, channels),
        in_weights,
    )


def gate_kernel(x_ref, gain_ref, bias_ref, w_ref, out_ref):
    rows, cols, channels = x_ref.shape
    values = x_ref[...].astype(jnp.float32).reshape(rows * cols, channels)
    normed = normalise(values, gain_ref[...], bias_ref[...]).astype(jnp.bfloat16)
    out_ref[...] = gated(contract(normed, w_ref[...], 1, 0), 1.0).reshape(rows, cols, channels)


def gates(pair_rep, in_gain, in_bias, gate_weight):
    rows, cols, channels = pair_rep.shape
    part = 16
    block = pl.BlockSpec((part, cols, channels), lambda s: (s, 0, 0))
    return pl.pallas_call(
        gate_kernel,
        grid=(rows // part,),
        in_specs=[block, fixed((1, channels)), fixed((1, channels)), fixed(gate_weight.shape)],
        out_specs=block,
        out_shape=jax.ShapeDtypeStruct((rows, cols, channels), jnp.float32),
        compiler_params=pltpu.CompilerParams(vmem_limit_bytes=16 * 1024 * 1024),
        cost_estimate=pl.CostEstimate(
            flops=2 * rows * cols * channels * channels,
            bytes_accessed=6 * rows * cols * channels,
            transcendentals=rows * cols * channels,
        ),
        name="gates",
    )(pair_rep, in_gain.reshape(1, channels), in_bias.reshape(1, channels), gate_weight)


def blocks(ref, which, zl):
    return jnp.concatenate(
        [
            ref[PLACE[zl + 4 * zh, x, y], which] if which is not None else ref[PLACE[zl + 4 * zh, x, y]]
            for x in range(4)
            for zh in range(2)
            for y in range(4)
        ],
        axis=0,
    )


def half_kernel(both_ref, out_ref):
    lefts = jnp.concatenate([blocks(both_ref, 0, zl) for zl in range(4)], axis=1)
    rights = jnp.concatenate([blocks(both_ref, 1, zl) for zl in range(4)], axis=1)
    out_ref[...] = contract(rights, lefts, 0, 0).astype(jnp.bfloat16)


def product_kernel(core_index, both_ref, right_ref, half_ref, out_ref):
    cols, wide = right_ref.shape[1:]
    core = core_index()
    lefts = jnp.concatenate([blocks(both_ref, 0, zl) for zl in range(4)], axis=1)
    rights = jnp.concatenate([blocks(right_ref, None, zl) for zl in range(4)], axis=1)
    out = contract(rights, lefts, 0, 0).astype(jnp.bfloat16)
    for zl in range(4):
        for x in range(4):
            for y in range(4):
                low, high = PLACE[zl, x, y], PLACE[zl + 4, x, y]
                place = (pl.ds(x * wide + y * cols, cols), pl.ds(zl * wide, wide))
                out_ref[low + core * (high - low)] = half_ref[place]
                out_ref[high + core * (low - high)] = out[
                    x * wide + y * cols : x * wide + (y + 1) * cols, zl * wide : (zl + 1) * wide
                ]


def half(both):
    rows = both.shape[3]
    whole = pl.BlockSpec(memory_space=pltpu.VMEM)
    return pl.pallas_call(
        half_kernel,
        in_specs=[whole],
        out_specs=whole,
        out_shape=jax.ShapeDtypeStruct((4 * rows, 4 * rows), jnp.bfloat16),
        compiler_params=pltpu.CompilerParams(vmem_limit_bytes=24 * 1024 * 1024),
        cost_estimate=pl.CostEstimate(
            flops=2 * 512 * 512 * 1024, bytes_accessed=5 << 19, transcendentals=0
        ),
        name="half",
    )(both)


def product(both, right, own, core=core_of):
    whole = pl.BlockSpec(memory_space=pltpu.VMEM)
    return pl.pallas_call(
        functools.partial(product_kernel, core),
        in_specs=[whole, whole, whole],
        out_specs=whole,
        out_shape=jax.ShapeDtypeStruct(right.shape, jnp.bfloat16),
        compiler_params=pltpu.CompilerParams(vmem_limit_bytes=24 * 1024 * 1024),
        name="product",
    )(both, right, own)


def finish_kernel(t_ref, gate_ref, gain_ref, bias_ref, w_ref, out_hbm, out_ref, ts, os, sems):
    hidden, cols, rows = t_ref.shape
    channels = w_ref.shape[1]
    part = 16
    gain = jnp.broadcast_to(gain_ref[...], (rows, hidden)).T
    bias = jnp.broadcast_to(bias_ref[...], (rows, hidden)).T
    stores = []
    for n in range(cols // part):
        here = slice(n * part, (n + 1) * part)
        values = t_ref[:, here].astype(jnp.float32)
        for h in range(hidden):
            ts[h * APART : h * APART + part, :] = values[h]
        average = jnp.sum(values, axis=0) * (1.0 / hidden)
        centred = values - average[None]
        spread = jnp.sum(centred * centred, axis=0) * (1.0 / hidden)
        scale = lax.rsqrt(spread + 1e-05)
        for j in range(part):
            of_j = ts[pl.ds(j, hidden, stride=APART), :]
            normed = (of_j - average[j : j + 1]) * scale[j : j + 1] * gain + bias
            os[pl.ds(j, rows, stride=APART), :] = contract(
                normed.astype(jnp.bfloat16), w_ref[...], 0, 0
            )
        for i in range(rows):
            out_ref[i, here] = (
                os[i * APART : i * APART + part, :] * gate_ref[i, here]
            ).astype(jnp.bfloat16)
            if (i + 1) % 64 == 0:
                some = (pl.ds(i - 63, 64), pl.ds(n * part, part))
                stores.append(
                    pltpu.make_async_copy(
                        out_ref.at[some], out_hbm.at[some], sems.at[len(stores)]
                    )
                )
                stores[-1].start()
    for store in stores:
        store.wait()


def finish(triangle, gate, out_gain, out_bias, out_weight):
    hidden, cols, rows = triangle.shape
    channels = out_weight.shape[1]
    part = 16
    whole = pl.BlockSpec(memory_space=pltpu.VMEM)
    return pl.pallas_call(
        finish_kernel,
        in_specs=[whole] * 5,
        out_specs=pl.BlockSpec(memory_space=pltpu.HBM),
        out_shape=jax.ShapeDtypeStruct((rows, cols, channels), jnp.bfloat16),
        scratch_shapes=[
            pltpu.VMEM((rows, cols, channels), jnp.bfloat16),
            pltpu.VMEM((hidden * APART, rows), jnp.float32),
            pltpu.VMEM((rows * APART, channels), jnp.float32),
            pltpu.SemaphoreType.DMA((2 * (cols // part),)),
        ],
        compiler_params=pltpu.CompilerParams(vmem_limit_bytes=32 * 1024 * 1024),
        name="finish",
    )(
        triangle,
        gate,
        out_gain.reshape(1, hidden),
        out_bias.reshape(1, hidden),
        out_weight,
    )


def swap(chunks):
    return lax.all_to_all(
        chunks, AXES, split_axis=0, concat_axis=0, tiled=True, axis_index_groups=GROUPS
    )


def local(
    pair_rep,
    residue_mask,
    in_gain,
    in_bias,
    in_weights,
    gate_weight,
    out_gain,
    out_bias,
    out_weight,
):
    rows, cols, channels = pair_rep.shape
    hidden = in_weights.shape[2]
    both = factors(pair_rep, residue_mask, in_gain, in_bias, in_weights)
    both, late = lax.optimization_barrier((both, pair_rep))
    both = swap(both.reshape(hidden, 2 * cols, rows)).reshape(hidden, 2, cols, rows)
    gate = gates(late, in_gain, in_bias, gate_weight)
    both, gate = lax.optimization_barrier((both, gate))
    other = lax.ppermute(both[:, 1], "core", [(0, 1), (1, 0)])
    own = half(both)
    triangle = swap(product(both, other, own))
    return finish(triangle, gate, out_gain, out_bias, out_weight)


def solution(mesh):
    fine = Mesh(mesh.devices.reshape(4, 2, 4, 2, 4), AXES)
    tile = P(("zl", "core"), ("x", "zh", "y"), None)
    placed = (tile, P(), P(), P(), P(), P(), P(), P(), P())
    return jax.shard_map(local, mesh=fine, in_specs=placed, out_specs=tile, check_vma=False)
```

```python
import functools

import jax
import jax.numpy as jnp
from jax import lax
from jax.experimental import pallas as pl
from jax.experimental.pallas import tpu as pltpu
from jax.sharding import Mesh
from jax.sharding import PartitionSpec as P

AXES = ("zl", "core", "x", "zh", "y")
ORDER = ("z1", "x1", "y1", "z2", "z0", "x0", "y0")
VMEM_LIMIT = 60 * 1024 * 1024
APART = 17


def chips():
    places = []
    for place in range(1 << len(ORDER)):
        at = {"z": 0, "x": 0, "y": 0}
        for n, (axis, bit) in enumerate(ORDER):
            at[axis] |= ((place >> (len(ORDER) - 1 - n)) & 1) << int(bit)
        places.append((7 - at["z"], 3 - at["x"], 3 - at["y"]))
    return places


CHIPS = chips()
PLACE = {chip: place for place, chip in enumerate(CHIPS)}
GROUPS = [
    [(((z % 4 * 2 + core) * 4 + x) * 2 + z // 4) * 4 + y for z, x, y in CHIPS] for core in range(2)
]


def contract(lhs, rhs, lhs_dim, rhs_dim):
    return lax.dot_general(
        lhs, rhs, (((lhs_dim,), (rhs_dim,)), ((), ())), preferred_element_type=jnp.float32
    )


def gated(gate, value):
    return value / (1.0 + jnp.exp(-gate))


def normalise(values, gain_row, bias_row):
    average = jnp.mean(values, axis=-1, keepdims=True)
    centred = values - average
    spread = jnp.mean(centred * centred, axis=-1, keepdims=True)
    return centred * lax.rsqrt(spread + 1e-05) * gain_row + bias_row


def factors_kernel(
    row_index, col_index, mask_ref, mask_row_ref, x_hbm, gain_ref, bias_ref, w_hbm, out_hbm, x_ref, w_ref, out_ref, xs, ls, rs, sems
):
    rows, cols, channels = x_hbm.shape
    hidden = w_hbm.shape[2]
    part = 16
    parts = cols // part
    copies = [
        pltpu.make_async_copy(
            x_hbm.at[:, pl.ds(n * part, part)], x_ref.at[n], sems.at[n]
        )
        for n in range(parts)
    ]
    load_w = pltpu.make_async_copy(w_hbm, w_ref, sems.at[parts])
    load_w.start()
    for copy in copies:
        copy.start()
    load_w.wait()
    weights = jnp.concatenate([w_ref[m].T for m in range(4)], axis=0)
    stores = []
    row_mask = mask_row_ref[pl.ds(row_index(), 1), :].astype(jnp.float32)
    first_col = col_index() * cols
    for n in range(parts):
        copies[n].wait()
        for first in range(0, rows, 16):
            piece = x_ref[n, first : first + 16].astype(jnp.float32).reshape(16 * part, channels)
            normed = normalise(piece, gain_ref[...], bias_ref[...])
            for i in range(16):
                xs[(first + i) * APART : (first + i) * APART + part, :] = normed[i * part : (i + 1) * part]
        for k in range(0, part, 2):
            of_k = jnp.concatenate(
                [xs[pl.ds(k + d, rows, stride=APART), :].astype(jnp.bfloat16) for d in range(2)],
                axis=0,
            )
            for side, kept in ((0, ls), (1, rs)):
                projected = contract(weights[2 * side * hidden : 2 * (side + 1) * hidden], of_k, 1, 1)
                for d in range(2):
                    mine = projected[:, d * rows : (d + 1) * rows]
                    mask = row_mask * mask_ref[first_col + n * part + k + d].astype(jnp.float32)
                    kept[pl.ds(k + d, hidden, stride=APART), :] = (
                        gated(mine[:hidden], mine[hidden:]) * mask
                    )
        here = slice(n * part, (n + 1) * part)
        for h in range(hidden):
            out_ref[h, 0, here] = ls[h * APART : h * APART + part].astype(jnp.bfloat16)
            out_ref[h, 1, here] = rs[h * APART : h * APART + part].astype(jnp.bfloat16)
        stores.append(
            pltpu.make_async_copy(
                out_ref.at[:, :, pl.ds(n * part, part)],
                out_hbm.at[:, :, pl.ds(n * part, part)],
                sems.at[parts + 1 + n],
            )
        )
        stores[-1].start()
    for store in stores:
        store.wait()


def row_of():
    return lax.axis_index("zl") * 2 + lax.axis_index("core")


def col_of():
    return (lax.axis_index("x") * 2 + lax.axis_index("zh")) * 4 + lax.axis_index("y")


def core_of():
    return lax.axis_index("core")


def fixed(shape):
    return pl.BlockSpec(shape, lambda s: (0,) * len(shape))


def factors(pair_rep, residue_mask, in_gain, in_bias, in_weights, row=row_of, col=col_of):
    rows, cols, channels = pair_rep.shape
    hidden = in_weights.shape[2]
    part = 16
    whole = pl.BlockSpec(memory_space=pltpu.VMEM)
    far = pl.BlockSpec(memory_space=pltpu.HBM)
    return pl.pallas_call(
        functools.partial(factors_kernel, row, col),
        in_specs=[pl.BlockSpec(memory_space=pltpu.SMEM), whole, far, whole, whole, far],
        out_specs=far,
        out_shape=jax.ShapeDtypeStruct((hidden, 2, cols, rows), jnp.bfloat16),
        scratch_shapes=[
            pltpu.VMEM((cols // part, rows, part, channels), jnp.bfloat16),
            pltpu.VMEM(in_weights.shape, jnp.bfloat16),
            pltpu.VMEM((hidden, 2, cols, rows), jnp.bfloat16),
            pltpu.VMEM(((rows + 1) * APART, channels), jnp.float32),
            pltpu.VMEM(((hidden + 1) * APART, rows), jnp.float32),
            pltpu.VMEM(((hidden + 1) * APART, rows), jnp.float32),
            pltpu.SemaphoreType.DMA((2 * (cols // part) + 1,)),
        ],
        compiler_params=pltpu.CompilerParams(vmem_limit_bytes=VMEM_LIMIT),
        name="factors",
    )(
        residue_mask,
        residue_mask.reshape(-1, rows),
        pair_rep,
        in_gain.reshape(1, channels),
        in_bias.reshape(1, channels),
        in_weights,
    )


def gate_kernel(x_ref, gain_ref, bias_ref, w_ref, out_ref):
    rows, cols, channels = x_ref.shape
    values = x_ref[...].astype(jnp.float32).reshape(rows * cols, channels)
    normed = normalise(values, gain_ref[...], bias_ref[...]).astype(jnp.bfloat16)
    out_ref[...] = gated(contract(normed, w_ref[...], 1, 0), 1.0).reshape(rows, cols, channels)


def gates(pair_rep, in_gain, in_bias, gate_weight):
    rows, cols, channels = pair_rep.shape
    part = 16
    block = pl.BlockSpec((part, cols, channels), lambda s: (s, 0, 0))
    return pl.pallas_call(
        gate_kernel,
        grid=(rows // part,),
        in_specs=[block, fixed((1, channels)), fixed((1, channels)), fixed(gate_weight.shape)],
        out_specs=block,
        out_shape=jax.ShapeDtypeStruct((rows, cols, channels), jnp.float32),
        compiler_params=pltpu.CompilerParams(vmem_limit_bytes=16 * 1024 * 1024),
        cost_estimate=pl.CostEstimate(
            flops=2 * rows * cols * channels * channels,
            bytes_accessed=6 * rows * cols * channels,
            transcendentals=rows * cols * channels,
        ),
        name="gates",
    )(pair_rep, in_gain.reshape(1, channels), in_bias.reshape(1, channels), gate_weight)


def blocks(ref, which, zl):
    return jnp.concatenate(
        [
            ref[PLACE[zl + 4 * zh, x, y], which] if which is not None else ref[PLACE[zl + 4 * zh, x, y]]
            for x in range(4)
            for zh in range(2)
            for y in range(4)
        ],
        axis=0,
    )


def half_kernel(both_ref, out_ref):
    lefts = jnp.concatenate([blocks(both_ref, 0, zl) for zl in range(4)], axis=1)
    rights = jnp.concatenate([blocks(both_ref, 1, zl) for zl in range(4)], axis=1)
    out_ref[...] = contract(rights, lefts, 0, 0).astype(jnp.bfloat16)


def product_kernel(core_index, both_ref, right_ref, half_ref, out_ref):
    cols, wide = right_ref.shape[1:]
    core = core_index()
    lefts = jnp.concatenate([blocks(both_ref, 0, zl) for zl in range(4)], axis=1)
    rights = jnp.concatenate([blocks(right_ref, None, zl) for zl in range(4)], axis=1)
    out = contract(rights, lefts, 0, 0).astype(jnp.bfloat16)
    for zl in range(4):
        for x in range(4):
            for y in range(4):
                low, high = PLACE[zl, x, y], PLACE[zl + 4, x, y]
                place = (pl.ds(x * wide + y * cols, cols), pl.ds(zl * wide, wide))
                out_ref[low + core * (high - low)] = half_ref[place]
                out_ref[high + core * (low - high)] = out[
                    x * wide + y * cols : x * wide + (y + 1) * cols, zl * wide : (zl + 1) * wide
                ]


def half(both):
    rows = both.shape[3]
    whole = pl.BlockSpec(memory_space=pltpu.VMEM)
    return pl.pallas_call(
        half_kernel,
        in_specs=[whole],
        out_specs=whole,
        out_shape=jax.ShapeDtypeStruct((4 * rows, 4 * rows), jnp.bfloat16),
        compiler_params=pltpu.CompilerParams(vmem_limit_bytes=24 * 1024 * 1024),
        cost_estimate=pl.CostEstimate(
            flops=2 * 512 * 512 * 1024, bytes_accessed=5 << 19, transcendentals=0
        ),
        name="half",
    )(both)


def product(both, right, own, core=core_of):
    whole = pl.BlockSpec(memory_space=pltpu.VMEM)
    return pl.pallas_call(
        functools.partial(product_kernel, core),
        in_specs=[whole, whole, whole],
        out_specs=whole,
        out_shape=jax.ShapeDtypeStruct(right.shape, jnp.bfloat16),
        compiler_params=pltpu.CompilerParams(vmem_limit_bytes=24 * 1024 * 1024),
        name="product",
    )(both, right, own)


def finish_kernel(t_ref, gate_ref, gain_ref, bias_ref, w_ref, out_hbm, out_ref, ts, os, sems):
    hidden, cols, rows = t_ref.shape
    channels = w_ref.shape[1]
    part = 16
    gain = jnp.broadcast_to(gain_ref[...], (rows, hidden)).T
    bias = jnp.broadcast_to(bias_ref[...], (rows, hidden)).T
    stores = []
    for n in range(cols // part):
        here = slice(n * part, (n + 1) * part)
        values = t_ref[:, here].astype(jnp.float32)
        for h in range(hidden):
            ts[h * APART : h * APART + part, :] = values[h]
        average = jnp.sum(values, axis=0) * (1.0 / hidden)
        centred = values - average[None]
        spread = jnp.sum(centred * centred, axis=0) * (1.0 / hidden)
        scale = lax.rsqrt(spread + 1e-05)
        for j in range(part):
            of_j = ts[pl.ds(j, hidden, stride=APART), :]
            normed = (of_j - average[j : j + 1]) * scale[j : j + 1] * gain + bias
            os[pl.ds(j, rows, stride=APART), :] = contract(
                normed.astype(jnp.bfloat16), w_ref[...], 0, 0
            )
        for i in range(rows):
            out_ref[i, here] = (
                os[i * APART : i * APART + part, :] * gate_ref[i, here]
            ).astype(jnp.bfloat16)
            if (i + 1) % 64 == 0:
                some = (pl.ds(i - 63, 64), pl.ds(n * part, part))
                stores.append(
                    pltpu.make_async_copy(
                        out_ref.at[some], out_hbm.at[some], sems.at[len(stores)]
                    )
                )
                stores[-1].start()
    for store in stores:
        store.wait()


def finish(triangle, gate, out_gain, out_bias, out_weight):
    hidden, cols, rows = triangle.shape
    channels = out_weight.shape[1]
    part = 16
    whole = pl.BlockSpec(memory_space=pltpu.VMEM)
    return pl.pallas_call(
        finish_kernel,
        in_specs=[whole] * 5,
        out_specs=pl.BlockSpec(memory_space=pltpu.HBM),
        out_shape=jax.ShapeDtypeStruct((rows, cols, channels), jnp.bfloat16),
        scratch_shapes=[
            pltpu.VMEM((rows, cols, channels), jnp.bfloat16),
            pltpu.VMEM(((hidden + 1) * APART, rows), jnp.float32),
            pltpu.VMEM(((rows + 1) * APART, channels), jnp.float32),
            pltpu.SemaphoreType.DMA((2 * (cols // part),)),
        ],
        compiler_params=pltpu.CompilerParams(vmem_limit_bytes=32 * 1024 * 1024),
        name="finish",
    )(
        triangle,
        gate,
        out_gain.reshape(1, hidden),
        out_bias.reshape(1, hidden),
        out_weight,
    )


def swap(chunks):
    return lax.all_to_all(
        chunks, AXES, split_axis=0, concat_axis=0, tiled=True, axis_index_groups=GROUPS
    )


def local(
    pair_rep,
    residue_mask,
    in_gain,
    in_bias,
    in_weights,
    gate_weight,
    out_gain,
    out_bias,
    out_weight,
):
    rows, cols, channels = pair_rep.shape
    hidden = in_weights.shape[2]
    both = factors(pair_rep, residue_mask, in_gain, in_bias, in_weights)
    both, late = lax.optimization_barrier((both, pair_rep))
    both = swap(both.reshape(hidden, 2 * cols, rows)).reshape(hidden, 2, cols, rows)
    gate = gates(late, in_gain, in_bias, gate_weight)
    both, gate = lax.optimization_barrier((both, gate))
    other = lax.ppermute(both[:, 1], "core", [(0, 1), (1, 0)])
    own = half(both)
    triangle = swap(product(both, other, own))
    return finish(triangle, gate, out_gain, out_bias, out_weight)


def solution(mesh):
    fine = Mesh(mesh.devices.reshape(4, 2, 4, 2, 4), AXES)
    tile = P(("zl", "core"), ("x", "zh", "y"), None)
    placed = (tile, P(), P(), P(), P(), P(), P(), P(), P())
    return jax.shard_map(local, mesh=fine, in_specs=placed, out_specs=tile, check_vma=False)
```

```python
import functools

import jax
import jax.numpy as jnp
from jax import lax
from jax.experimental import pallas as pl
from jax.experimental.pallas import tpu as pltpu
from jax.sharding import Mesh
from jax.sharding import PartitionSpec as P

AXES = ("zl", "core", "x", "zh", "y")
ORDER = ("z1", "y1", "x1", "z2", "z0", "y0", "x0")
VMEM_LIMIT = 60 * 1024 * 1024
APART = 17


def chips():
    places = []
    for place in range(1 << len(ORDER)):
        at = {"z": 0, "x": 0, "y": 0}
        for n, (axis, bit) in enumerate(ORDER):
            at[axis] |= ((place >> (len(ORDER) - 1 - n)) & 1) << int(bit)
        places.append((7 - at["z"], 3 - at["x"], 3 - at["y"]))
    return places


CHIPS = chips()
PLACE = {chip: place for place, chip in enumerate(CHIPS)}
GROUPS = [
    [(((z % 4 * 2 + core) * 4 + x) * 2 + z // 4) * 4 + y for z, x, y in CHIPS] for core in range(2)
]


def contract(lhs, rhs, lhs_dim, rhs_dim):
    return lax.dot_general(
        lhs, rhs, (((lhs_dim,), (rhs_dim,)), ((), ())), preferred_element_type=jnp.float32
    )


def gated(gate, value):
    return value / (1.0 + jnp.exp(-gate))


def normalise(values, gain_row, bias_row):
    average = jnp.mean(values, axis=-1, keepdims=True)
    centred = values - average
    spread = jnp.mean(centred * centred, axis=-1, keepdims=True)
    return centred * lax.rsqrt(spread + 1e-05) * gain_row + bias_row


def factors_kernel(
    row_index, col_index, mask_ref, mask_row_ref, x_hbm, gain_ref, bias_ref, w_hbm, out_hbm, x_ref, w_ref, out_ref, xs, ls, rs, sems
):
    rows, cols, channels = x_hbm.shape
    hidden = w_hbm.shape[2]
    part = 16
    parts = cols // part
    copies = [
        pltpu.make_async_copy(
            x_hbm.at[:, pl.ds(n * part, part)], x_ref.at[n], sems.at[n]
        )
        for n in range(parts)
    ]
    load_w = pltpu.make_async_copy(w_hbm, w_ref, sems.at[parts])
    load_w.start()
    for copy in copies:
        copy.start()
    load_w.wait()
    weights = jnp.concatenate([w_ref[m].T for m in range(4)], axis=0)
    stores = []
    row_mask = mask_row_ref[pl.ds(row_index(), 1), :].astype(jnp.float32)
    first_col = col_index() * cols
    for n in range(parts):
        copies[n].wait()
        for first in range(0, rows, 16):
            piece = x_ref[n, first : first + 16].astype(jnp.float32).reshape(16 * part, channels)
            normed = normalise(piece, gain_ref[...], bias_ref[...])
            for i in range(16):
                xs[(first + i) * APART : (first + i) * APART + part, :] = normed[i * part : (i + 1) * part]
        for k in range(0, part, 2):
            of_k = jnp.concatenate(
                [xs[pl.ds(k + d, rows, stride=APART), :].astype(jnp.bfloat16) for d in range(2)],
                axis=0,
            )
            for side, kept in ((0, ls), (1, rs)):
                projected = contract(weights[2 * side * hidden : 2 * (side + 1) * hidden], of_k, 1, 1)
                for d in range(2):
                    mine = projected[:, d * rows : (d + 1) * rows]
                    mask = row_mask * mask_ref[first_col + n * part + k + d].astype(jnp.float32)
                    kept[pl.ds(k + d, hidden, stride=APART), :] = (
                        gated(mine[:hidden], mine[hidden:]) * mask
                    )
        here = slice(n * part, (n + 1) * part)
        for h in range(hidden):
            out_ref[h, 0, here] = ls[h * APART : h * APART + part].astype(jnp.bfloat16)
            out_ref[h, 1, here] = rs[h * APART : h * APART + part].astype(jnp.bfloat16)
        stores.append(
            pltpu.make_async_copy(
                out_ref.at[:, :, pl.ds(n * part, part)],
                out_hbm.at[:, :, pl.ds(n * part, part)],
                sems.at[parts + 1 + n],
            )
        )
        stores[-1].start()
    for store in stores:
        store.wait()


def row_of():
    return lax.axis_index("zl") * 2 + lax.axis_index("core")


def col_of():
    return (lax.axis_index("x") * 2 + lax.axis_index("zh")) * 4 + lax.axis_index("y")


def core_of():
    return lax.axis_index("core")


def fixed(shape):
    return pl.BlockSpec(shape, lambda s: (0,) * len(shape))


def factors(pair_rep, residue_mask, in_gain, in_bias, in_weights, row=row_of, col=col_of):
    rows, cols, channels = pair_rep.shape
    hidden = in_weights.shape[2]
    part = 16
    whole = pl.BlockSpec(memory_space=pltpu.VMEM)
    far = pl.BlockSpec(memory_space=pltpu.HBM)
    return pl.pallas_call(
        functools.partial(factors_kernel, row, col),
        in_specs=[pl.BlockSpec(memory_space=pltpu.SMEM), whole, far, whole, whole, far],
        out_specs=far,
        out_shape=jax.ShapeDtypeStruct((hidden, 2, cols, rows), jnp.bfloat16),
        scratch_shapes=[
            pltpu.VMEM((cols // part, rows, part, channels), jnp.bfloat16),
            pltpu.VMEM(in_weights.shape, jnp.bfloat16),
            pltpu.VMEM((hidden, 2, cols, rows), jnp.bfloat16),
            pltpu.VMEM(((rows + 1) * APART, channels), jnp.float32),
            pltpu.VMEM(((hidden + 1) * APART, rows), jnp.float32),
            pltpu.VMEM(((hidden + 1) * APART, rows), jnp.float32),
            pltpu.SemaphoreType.DMA((2 * (cols // part) + 1,)),
        ],
        compiler_params=pltpu.CompilerParams(vmem_limit_bytes=VMEM_LIMIT),
        name="factors",
    )(
        residue_mask,
        residue_mask.reshape(-1, rows),
        pair_rep,
        in_gain.reshape(1, channels),
        in_bias.reshape(1, channels),
        in_weights,
    )


def gate_kernel(x_ref, gain_ref, bias_ref, w_ref, out_ref):
    rows, cols, channels = x_ref.shape
    values = x_ref[...].astype(jnp.float32).reshape(rows * cols, channels)
    normed = normalise(values, gain_ref[...], bias_ref[...]).astype(jnp.bfloat16)
    out_ref[...] = gated(contract(normed, w_ref[...], 1, 0), 1.0).reshape(rows, cols, channels)


def gates(pair_rep, in_gain, in_bias, gate_weight):
    rows, cols, channels = pair_rep.shape
    part = 16
    block = pl.BlockSpec((part, cols, channels), lambda s: (s, 0, 0))
    return pl.pallas_call(
        gate_kernel,
        grid=(rows // part,),
        in_specs=[block, fixed((1, channels)), fixed((1, channels)), fixed(gate_weight.shape)],
        out_specs=block,
        out_shape=jax.ShapeDtypeStruct((rows, cols, channels), jnp.float32),
        compiler_params=pltpu.CompilerParams(vmem_limit_bytes=16 * 1024 * 1024),
        cost_estimate=pl.CostEstimate(
            flops=2 * rows * cols * channels * channels,
            bytes_accessed=6 * rows * cols * channels,
            transcendentals=rows * cols * channels,
        ),
        name="gates",
    )(pair_rep, in_gain.reshape(1, channels), in_bias.reshape(1, channels), gate_weight)


def blocks(ref, which, zl):
    return jnp.concatenate(
        [
            ref[PLACE[zl + 4 * zh, x, y], which] if which is not None else ref[PLACE[zl + 4 * zh, x, y]]
            for x in range(4)
            for zh in range(2)
            for y in range(4)
        ],
        axis=0,
    )


def half_kernel(both_ref, out_ref):
    lefts = jnp.concatenate([blocks(both_ref, 0, zl) for zl in range(4)], axis=1)
    rights = jnp.concatenate([blocks(both_ref, 1, zl) for zl in range(4)], axis=1)
    out_ref[...] = contract(rights, lefts, 0, 0).astype(jnp.bfloat16)


def product_kernel(core_index, both_ref, right_ref, half_ref, out_ref):
    cols, wide = right_ref.shape[1:]
    core = core_index()
    lefts = jnp.concatenate([blocks(both_ref, 0, zl) for zl in range(4)], axis=1)
    rights = jnp.concatenate([blocks(right_ref, None, zl) for zl in range(4)], axis=1)
    out = contract(rights, lefts, 0, 0).astype(jnp.bfloat16)
    for zl in range(4):
        for x in range(4):
            for y in range(4):
                low, high = PLACE[zl, x, y], PLACE[zl + 4, x, y]
                place = (pl.ds(x * wide + y * cols, cols), pl.ds(zl * wide, wide))
                out_ref[low + core * (high - low)] = half_ref[place]
                out_ref[high + core * (low - high)] = out[
                    x * wide + y * cols : x * wide + (y + 1) * cols, zl * wide : (zl + 1) * wide
                ]


def half(both):
    rows = both.shape[3]
    whole = pl.BlockSpec(memory_space=pltpu.VMEM)
    return pl.pallas_call(
        half_kernel,
        in_specs=[whole],
        out_specs=whole,
        out_shape=jax.ShapeDtypeStruct((4 * rows, 4 * rows), jnp.bfloat16),
        compiler_params=pltpu.CompilerParams(vmem_limit_bytes=24 * 1024 * 1024),
        cost_estimate=pl.CostEstimate(
            flops=2 * 512 * 512 * 1024, bytes_accessed=5 << 19, transcendentals=0
        ),
        name="half",
    )(both)


def product(both, right, own, core=core_of):
    whole = pl.BlockSpec(memory_space=pltpu.VMEM)
    return pl.pallas_call(
        functools.partial(product_kernel, core),
        in_specs=[whole, whole, whole],
        out_specs=whole,
        out_shape=jax.ShapeDtypeStruct(right.shape, jnp.bfloat16),
        compiler_params=pltpu.CompilerParams(vmem_limit_bytes=24 * 1024 * 1024),
        name="product",
    )(both, right, own)


def finish_kernel(t_ref, gate_ref, gain_ref, bias_ref, w_ref, out_hbm, out_ref, ts, os, sems):
    hidden, cols, rows = t_ref.shape
    channels = w_ref.shape[1]
    part = 16
    gain = jnp.broadcast_to(gain_ref[...], (rows, hidden)).T
    bias = jnp.broadcast_to(bias_ref[...], (rows, hidden)).T
    stores = []
    for n in range(cols // part):
        here = slice(n * part, (n + 1) * part)
        values = t_ref[:, here].astype(jnp.float32)
        for h in range(hidden):
            ts[h * APART : h * APART + part, :] = values[h]
        average = jnp.sum(values, axis=0) * (1.0 / hidden)
        centred = values - average[None]
        spread = jnp.sum(centred * centred, axis=0) * (1.0 / hidden)
        scale = lax.rsqrt(spread + 1e-05)
        for j in range(part):
            of_j = ts[pl.ds(j, hidden, stride=APART), :]
            normed = (of_j - average[j : j + 1]) * scale[j : j + 1] * gain + bias
            os[pl.ds(j, rows, stride=APART), :] = contract(
                normed.astype(jnp.bfloat16), w_ref[...], 0, 0
            )
        for i in range(rows):
            out_ref[i, here] = (
                os[i * APART : i * APART + part, :] * gate_ref[i, here]
            ).astype(jnp.bfloat16)
            if (i + 1) % 64 == 0:
                some = (pl.ds(i - 63, 64), pl.ds(n * part, part))
                stores.append(
                    pltpu.make_async_copy(
                        out_ref.at[some], out_hbm.at[some], sems.at[len(stores)]
                    )
                )
                stores[-1].start()
    for store in stores:
        store.wait()


def finish(triangle, gate, out_gain, out_bias, out_weight):
    hidden, cols, rows = triangle.shape
    channels = out_weight.shape[1]
    part = 16
    whole = pl.BlockSpec(memory_space=pltpu.VMEM)
    return pl.pallas_call(
        finish_kernel,
        in_specs=[whole] * 5,
        out_specs=pl.BlockSpec(memory_space=pltpu.HBM),
        out_shape=jax.ShapeDtypeStruct((rows, cols, channels), jnp.bfloat16),
        scratch_shapes=[
            pltpu.VMEM((rows, cols, channels), jnp.bfloat16),
            pltpu.VMEM(((hidden + 1) * APART, rows), jnp.float32),
            pltpu.VMEM(((rows + 1) * APART, channels), jnp.float32),
            pltpu.SemaphoreType.DMA((2 * (cols // part),)),
        ],
        compiler_params=pltpu.CompilerParams(vmem_limit_bytes=32 * 1024 * 1024),
        name="finish",
    )(
        triangle,
        gate,
        out_gain.reshape(1, hidden),
        out_bias.reshape(1, hidden),
        out_weight,
    )


def swap(chunks):
    return lax.all_to_all(
        chunks, AXES, split_axis=0, concat_axis=0, tiled=True, axis_index_groups=GROUPS
    )


def local(
    pair_rep,
    residue_mask,
    in_gain,
    in_bias,
    in_weights,
    gate_weight,
    out_gain,
    out_bias,
    out_weight,
):
    rows, cols, channels = pair_rep.shape
    hidden = in_weights.shape[2]
    both = factors(pair_rep, residue_mask, in_gain, in_bias, in_weights)
    both, late = lax.optimization_barrier((both, pair_rep))
    both = swap(both.reshape(hidden, 2 * cols, rows)).reshape(hidden, 2, cols, rows)
    gate = gates(late, in_gain, in_bias, gate_weight)
    both, gate = lax.optimization_barrier((both, gate))
    other = lax.ppermute(both[:, 1], "core", [(0, 1), (1, 0)])
    own = half(both)
    triangle = swap(product(both, other, own))
    return finish(triangle, gate, out_gain, out_bias, out_weight)


def solution(mesh):
    fine = Mesh(mesh.devices.reshape(4, 2, 4, 2, 4), AXES)
    tile = P(("zl", "core"), ("x", "zh", "y"), None)
    placed = (tile, P(), P(), P(), P(), P(), P(), P(), P())
    return jax.shard_map(local, mesh=fine, in_specs=placed, out_specs=tile, check_vma=False)
```

```python
import functools

import jax
import jax.numpy as jnp
from jax import lax
from jax.experimental import pallas as pl
from jax.experimental.pallas import tpu as pltpu
from jax.sharding import Mesh
from jax.sharding import PartitionSpec as P

AXES = ("zl", "core", "x", "zh", "y")
ORDER = ("z0", "z1", "z2", "x0", "x1", "y0", "y1")
VMEM_LIMIT = 60 * 1024 * 1024
APART = 17


def chips():
    places = []
    for place in range(1 << len(ORDER)):
        at = {"z": 0, "x": 0, "y": 0}
        for n, (axis, bit) in enumerate(ORDER):
            at[axis] |= ((place >> (len(ORDER) - 1 - n)) & 1) << int(bit)
        places.append((7 - at["z"], 3 - at["x"], 3 - at["y"]))
    return places


CHIPS = chips()
PLACE = {chip: place for place, chip in enumerate(CHIPS)}
GROUPS = [
    [(((z % 4 * 2 + core) * 4 + x) * 2 + z // 4) * 4 + y for z, x, y in CHIPS] for core in range(2)
]


def contract(lhs, rhs, lhs_dim, rhs_dim):
    return lax.dot_general(
        lhs, rhs, (((lhs_dim,), (rhs_dim,)), ((), ())), preferred_element_type=jnp.float32
    )


def gated(gate, value):
    return value / (1.0 + jnp.exp(-gate))


def normalise(values, gain_row, bias_row):
    average = jnp.mean(values, axis=-1, keepdims=True)
    centred = values - average
    spread = jnp.mean(centred * centred, axis=-1, keepdims=True)
    return centred * lax.rsqrt(spread + 1e-05) * gain_row + bias_row


def factors_kernel(
    row_index, col_index, mask_ref, mask_row_ref, x_hbm, gain_ref, bias_ref, w_hbm, out_hbm, x_ref, w_ref, out_ref, xs, ls, rs, sems
):
    rows, cols, channels = x_hbm.shape
    hidden = w_hbm.shape[2]
    part = 16
    parts = cols // part
    copies = [
        pltpu.make_async_copy(
            x_hbm.at[:, pl.ds(n * part, part)], x_ref.at[n], sems.at[n]
        )
        for n in range(parts)
    ]
    load_w = pltpu.make_async_copy(w_hbm, w_ref, sems.at[parts])
    load_w.start()
    for copy in copies:
        copy.start()
    load_w.wait()
    weights = jnp.concatenate([w_ref[m].T for m in range(4)], axis=0)
    stores = []
    row_mask = mask_row_ref[pl.ds(row_index(), 1), :].astype(jnp.float32)
    first_col = col_index() * cols
    for n in range(parts):
        copies[n].wait()
        for first in range(0, rows, 16):
            piece = x_ref[n, first : first + 16].astype(jnp.float32).reshape(16 * part, channels)
            normed = normalise(piece, gain_ref[...], bias_ref[...])
            for i in range(16):
                xs[(first + i) * APART : (first + i) * APART + part, :] = normed[i * part : (i + 1) * part]
        for k in range(0, part, 2):
            of_k = jnp.concatenate(
                [xs[pl.ds(k + d, rows, stride=APART), :].astype(jnp.bfloat16) for d in range(2)],
                axis=0,
            )
            for side, kept in ((0, ls), (1, rs)):
                projected = contract(weights[2 * side * hidden : 2 * (side + 1) * hidden], of_k, 1, 1)
                for d in range(2):
                    mine = projected[:, d * rows : (d + 1) * rows]
                    mask = row_mask * mask_ref[first_col + n * part + k + d].astype(jnp.float32)
                    kept[pl.ds(k + d, hidden, stride=APART), :] = (
                        gated(mine[:hidden], mine[hidden:]) * mask
                    )
        here = slice(n * part, (n + 1) * part)
        for h in range(hidden):
            out_ref[h, 0, here] = ls[h * APART : h * APART + part].astype(jnp.bfloat16)
            out_ref[h, 1, here] = rs[h * APART : h * APART + part].astype(jnp.bfloat16)
        stores.append(
            pltpu.make_async_copy(
                out_ref.at[:, :, pl.ds(n * part, part)],
                out_hbm.at[:, :, pl.ds(n * part, part)],
                sems.at[parts + 1 + n],
            )
        )
        stores[-1].start()
    for store in stores:
        store.wait()


def row_of():
    return lax.axis_index("zl") * 2 + lax.axis_index("core")


def col_of():
    return (lax.axis_index("x") * 2 + lax.axis_index("zh")) * 4 + lax.axis_index("y")


def core_of():
    return lax.axis_index("core")


def fixed(shape):
    return pl.BlockSpec(shape, lambda s: (0,) * len(shape))


def factors(pair_rep, residue_mask, in_gain, in_bias, in_weights, row=row_of, col=col_of):
    rows, cols, channels = pair_rep.shape
    hidden = in_weights.shape[2]
    part = 16
    whole = pl.BlockSpec(memory_space=pltpu.VMEM)
    far = pl.BlockSpec(memory_space=pltpu.HBM)
    return pl.pallas_call(
        functools.partial(factors_kernel, row, col),
        in_specs=[pl.BlockSpec(memory_space=pltpu.SMEM), whole, far, whole, whole, far],
        out_specs=far,
        out_shape=jax.ShapeDtypeStruct((hidden, 2, cols, rows), jnp.bfloat16),
        scratch_shapes=[
            pltpu.VMEM((cols // part, rows, part, channels), jnp.bfloat16),
            pltpu.VMEM(in_weights.shape, jnp.bfloat16),
            pltpu.VMEM((hidden, 2, cols, rows), jnp.bfloat16),
            pltpu.VMEM(((rows + 1) * APART, channels), jnp.float32),
            pltpu.VMEM(((hidden + 1) * APART, rows), jnp.float32),
            pltpu.VMEM(((hidden + 1) * APART, rows), jnp.float32),
            pltpu.SemaphoreType.DMA((2 * (cols // part) + 1,)),
        ],
        compiler_params=pltpu.CompilerParams(vmem_limit_bytes=VMEM_LIMIT),
        name="factors",
    )(
        residue_mask,
        residue_mask.reshape(-1, rows),
        pair_rep,
        in_gain.reshape(1, channels),
        in_bias.reshape(1, channels),
        in_weights,
    )


def gate_kernel(x_ref, gain_ref, bias_ref, w_ref, out_ref):
    rows, cols, channels = x_ref.shape
    values = x_ref[...].astype(jnp.float32).reshape(rows * cols, channels)
    normed = normalise(values, gain_ref[...], bias_ref[...]).astype(jnp.bfloat16)
    out_ref[...] = gated(contract(normed, w_ref[...], 1, 0), 1.0).reshape(rows, cols, channels)


def gates(pair_rep, in_gain, in_bias, gate_weight):
    rows, cols, channels = pair_rep.shape
    part = 16
    block = pl.BlockSpec((part, cols, channels), lambda s: (s, 0, 0))
    return pl.pallas_call(
        gate_kernel,
        grid=(rows // part,),
        in_specs=[block, fixed((1, channels)), fixed((1, channels)), fixed(gate_weight.shape)],
        out_specs=block,
        out_shape=jax.ShapeDtypeStruct((rows, cols, channels), jnp.float32),
        compiler_params=pltpu.CompilerParams(vmem_limit_bytes=16 * 1024 * 1024),
        cost_estimate=pl.CostEstimate(
            flops=2 * rows * cols * channels * channels,
            bytes_accessed=6 * rows * cols * channels,
            transcendentals=rows * cols * channels,
        ),
        name="gates",
    )(pair_rep, in_gain.reshape(1, channels), in_bias.reshape(1, channels), gate_weight)


def blocks(ref, which, zl):
    return jnp.concatenate(
        [
            ref[PLACE[zl + 4 * zh, x, y], which] if which is not None else ref[PLACE[zl + 4 * zh, x, y]]
            for x in range(4)
            for zh in range(2)
            for y in range(4)
        ],
        axis=0,
    )


def half_kernel(both_ref, out_ref):
    lefts = jnp.concatenate([blocks(both_ref, 0, zl) for zl in range(4)], axis=1)
    rights = jnp.concatenate([blocks(both_ref, 1, zl) for zl in range(4)], axis=1)
    out_ref[...] = contract(rights, lefts, 0, 0).astype(jnp.bfloat16)


def product_kernel(core_index, both_ref, right_ref, half_ref, out_ref):
    cols, wide = right_ref.shape[1:]
    core = core_index()
    lefts = jnp.concatenate([blocks(both_ref, 0, zl) for zl in range(4)], axis=1)
    rights = jnp.concatenate([blocks(right_ref, None, zl) for zl in range(4)], axis=1)
    out = contract(rights, lefts, 0, 0).astype(jnp.bfloat16)
    for zl in range(4):
        for x in range(4):
            for y in range(4):
                low, high = PLACE[zl, x, y], PLACE[zl + 4, x, y]
                place = (pl.ds(x * wide + y * cols, cols), pl.ds(zl * wide, wide))
                out_ref[low + core * (high - low)] = half_ref[place]
                out_ref[high + core * (low - high)] = out[
                    x * wide + y * cols : x * wide + (y + 1) * cols, zl * wide : (zl + 1) * wide
                ]


def half(both):
    rows = both.shape[3]
    whole = pl.BlockSpec(memory_space=pltpu.VMEM)
    return pl.pallas_call(
        half_kernel,
        in_specs=[whole],
        out_specs=whole,
        out_shape=jax.ShapeDtypeStruct((4 * rows, 4 * rows), jnp.bfloat16),
        compiler_params=pltpu.CompilerParams(vmem_limit_bytes=24 * 1024 * 1024),
        cost_estimate=pl.CostEstimate(
            flops=2 * 512 * 512 * 1024, bytes_accessed=5 << 19, transcendentals=0
        ),
        name="half",
    )(both)


def product(both, right, own, core=core_of):
    whole = pl.BlockSpec(memory_space=pltpu.VMEM)
    return pl.pallas_call(
        functools.partial(product_kernel, core),
        in_specs=[whole, whole, whole],
        out_specs=whole,
        out_shape=jax.ShapeDtypeStruct(right.shape, jnp.bfloat16),
        compiler_params=pltpu.CompilerParams(vmem_limit_bytes=24 * 1024 * 1024),
        name="product",
    )(both, right, own)


def finish_kernel(t_ref, gate_ref, gain_ref, bias_ref, w_ref, out_hbm, out_ref, ts, os, sems):
    hidden, cols, rows = t_ref.shape
    channels = w_ref.shape[1]
    part = 16
    gain = jnp.broadcast_to(gain_ref[...], (rows, hidden)).T
    bias = jnp.broadcast_to(bias_ref[...], (rows, hidden)).T
    stores = []
    for n in range(cols // part):
        here = slice(n * part, (n + 1) * part)
        values = t_ref[:, here].astype(jnp.float32)
        for h in range(hidden):
            ts[h * APART : h * APART + part, :] = values[h]
        average = jnp.sum(values, axis=0) * (1.0 / hidden)
        centred = values - average[None]
        spread = jnp.sum(centred * centred, axis=0) * (1.0 / hidden)
        scale = lax.rsqrt(spread + 1e-05)
        for j in range(part):
            of_j = ts[pl.ds(j, hidden, stride=APART), :]
            normed = (of_j - average[j : j + 1]) * scale[j : j + 1] * gain + bias
            os[pl.ds(j, rows, stride=APART), :] = contract(
                normed.astype(jnp.bfloat16), w_ref[...], 0, 0
            )
        for i in range(rows):
            out_ref[i, here] = (
                os[i * APART : i * APART + part, :] * gate_ref[i, here]
            ).astype(jnp.bfloat16)
            if (i + 1) % 64 == 0:
                some = (pl.ds(i - 63, 64), pl.ds(n * part, part))
                stores.append(
                    pltpu.make_async_copy(
                        out_ref.at[some], out_hbm.at[some], sems.at[len(stores)]
                    )
                )
                stores[-1].start()
    for store in stores:
        store.wait()


def finish(triangle, gate, out_gain, out_bias, out_weight):
    hidden, cols, rows = triangle.shape
    channels = out_weight.shape[1]
    part = 16
    whole = pl.BlockSpec(memory_space=pltpu.VMEM)
    return pl.pallas_call(
        finish_kernel,
        in_specs=[whole] * 5,
        out_specs=pl.BlockSpec(memory_space=pltpu.HBM),
        out_shape=jax.ShapeDtypeStruct((rows, cols, channels), jnp.bfloat16),
        scratch_shapes=[
            pltpu.VMEM((rows, cols, channels), jnp.bfloat16),
            pltpu.VMEM(((hidden + 1) * APART, rows), jnp.float32),
            pltpu.VMEM(((rows + 1) * APART, channels), jnp.float32),
            pltpu.SemaphoreType.DMA((2 * (cols // part),)),
        ],
        compiler_params=pltpu.CompilerParams(vmem_limit_bytes=32 * 1024 * 1024),
        name="finish",
    )(
        triangle,
        gate,
        out_gain.reshape(1, hidden),
        out_bias.reshape(1, hidden),
        out_weight,
    )


def swap(chunks):
    return lax.all_to_all(
        chunks, AXES, split_axis=0, concat_axis=0, tiled=True, axis_index_groups=GROUPS
    )


def local(
    pair_rep,
    residue_mask,
    in_gain,
    in_bias,
    in_weights,
    gate_weight,
    out_gain,
    out_bias,
    out_weight,
):
    rows, cols, channels = pair_rep.shape
    hidden = in_weights.shape[2]
    both = factors(pair_rep, residue_mask, in_gain, in_bias, in_weights)
    both, late = lax.optimization_barrier((both, pair_rep))
    both = swap(both.reshape(hidden, 2 * cols, rows)).reshape(hidden, 2, cols, rows)
    gate = gates(late, in_gain, in_bias, gate_weight)
    both, gate = lax.optimization_barrier((both, gate))
    other = lax.ppermute(both[:, 1], "core", [(0, 1), (1, 0)])
    own = half(both)
    triangle = swap(product(both, other, own))
    return finish(triangle, gate, out_gain, out_bias, out_weight)


def solution(mesh):
    fine = Mesh(mesh.devices.reshape(4, 2, 4, 2, 4), AXES)
    tile = P(("zl", "core"), ("x", "zh", "y"), None)
    placed = (tile, P(), P(), P(), P(), P(), P(), P(), P())
    return jax.shard_map(local, mesh=fine, in_specs=placed, out_specs=tile, check_vma=False)
```
